32 devices in a mesh: date: 8 (over y, x, core), swath: 4 (over z).
Axes of the slice: x: 2, y: 2, z: 4, core: 2. Of those that a mesh axis runs over, the one named last changes fastest.
Arguments:
- raw_echo: bfloat16 [8, 2, 1024, 2048], P('date', None, 'swath'), may hold values from -8 to 8
- range_rate: float32 [], replicated, may hold values from 0.5 to 1
- azimuth_rate: float32 [2048], P('swath'), may hold values from 0.25 to 1
- line_offset: int32 [8], P('date'), may hold values from 0 to 24, as said below
- frac_shift: float32 [8], P('date'), may hold values from 0 to 1
Outputs:
- coregistered: bfloat16 [8, 2, 1024, 2048], P('date', None, 'swath')
- coherence: bfloat16 [8, 2, 2, 1024, 2048], P('date', None, None, 'swath')
The draws below stay inside these ranges and needn't reach their ends.
Inputs may be any that keep to these rules, and one draw needn't show every extreme that they name: `line_offset`: one date has offset 24 and another has offset 0.
All inputs are finite; a program needn't handle non-finite values.
Results may differ from the reference program's by a relative error of at most 0.0076.
Values may be sent and summed in bfloat16 or wider, within the bound.
No kernel may reach another device: no remote copies, remote signals or barrier semaphores. Data moves between devices by JAX's collectives and lax.ppermute only.
A program may use at most 128 MiB of HBM per device.

```python
import math
import jax
import jax.numpy as jnp
from jax import lax

AZ = 1024
RG = 2048
TAPS = 8
MAX_OFF = 24
WIN_AZ = 11
WIN_RG = 5
SPAN = 2
DATES = 8


def offsets_from(key):
    first_key, second_key = jax.random.split(jax.random.fold_in(key, 5))
    drawn = jax.random.randint(first_key, (DATES,), 0, MAX_OFF + 1, dtype=jnp.int32)
    shuffled = jax.random.permutation(second_key, DATES)
    drawn = drawn.at[shuffled[0]].set(MAX_OFF)
    return drawn.at[shuffled[1]].set(0)


def draw_line_offset(key, part):
    return offsets_from(key)


def draw_raw_echo(key, part):
    offsets = offsets_from(key)
    scene_key, noise_key, turn_key = jax.random.split(jax.random.fold_in(key, 9), 3)
    scene_part = jax.random.normal(scene_key, (2, AZ, RG), jnp.float32)
    noise_part = jax.random.normal(noise_key, (DATES, 2, AZ, RG), jnp.float32)
    coherent_weight = 0.8
    noise_weight = math.sqrt(1.0 - coherent_weight * coherent_weight)
    turn_angles = jax.random.uniform(turn_key, (DATES,), jnp.float32, -math.pi, math.pi)

    def place(line_shift, turn_angle):
        rolled = jnp.roll(scene_part, line_shift, axis=1)
        cosine = jnp.cos(turn_angle)
        sine_val = jnp.sin(turn_angle)
        return jnp.stack([cosine * rolled[0] - sine_val * rolled[1], sine_val * rolled[0] + cosine * rolled[1]])
    aligned = jax.vmap(place)(offsets, turn_angles)
    blended = coherent_weight * aligned + noise_weight * noise_part
    return jnp.clip(blended, -8.0, 8.0).astype(jnp.bfloat16)


def block_levels(own_key, shape, cuts, least, largest):
    loudness, own = 1.0, jax.random.fold_in(own_key, 6)
    for dim, shards_of in cuts:
        draws = jnp.exp(jax.random.uniform(jax.random.fold_in(own, dim), (shards_of,), jnp.float32, least / len(cuts), largest / len(cuts)))
        loudness = loudness * jnp.repeat(draws, shape[dim] // shards_of).reshape([-1 if axis == dim else 1 for axis in range(len(shape))])
    return loudness


def setup_inputs(seed: int = 0) -> dict:
    key_of = jax.random.split(jax.random.key(seed), 6)
    return {
        "raw_echo": draw_raw_echo(jax.random.fold_in(key_of[5], 71), 0),
        "range_rate": jnp.clip(jax.random.uniform(key_of[1], (), jnp.float32, 0.5, 1.0), 0.5, 1.0),
        "azimuth_rate": jnp.clip(jnp.exp(math.log(1.0) - 1.3862944 * jax.random.uniform(key_of[2], (RG,), jnp.float32) ** block_levels(key_of[2], (RG,), ((0, 4),), -0.2, 0.2)), 0.25, 1.0),
        "line_offset": draw_line_offset(jax.random.fold_in(key_of[5], 71), 0),
        "frac_shift": jnp.clip(1.0 * jax.random.uniform(key_of[4], (DATES,), jnp.float32) ** block_levels(key_of[4], (DATES,), ((0, 8),), -0.2, 0.2), 0.0, 1.0),
    }


two_pi = 2.0 * math.pi
epsilon = 1e-06

def exact_dot(left, right):
    return jnp.dot(left.astype(jnp.float32), right.astype(jnp.float32), precision=lax.Precision.HIGHEST, preferred_element_type=jnp.float32)

def chirp_block(range_rate, row_count, col_count):
    pulse_len = RG // 2
    row_ids = lax.broadcasted_iota(jnp.int32, (row_count, col_count), 0)
    col_ids = lax.broadcasted_iota(jnp.int32, (row_count, col_count), 1)
    lag_ids = row_ids - col_ids
    inside = (lag_ids >= 0) & (lag_ids < pulse_len)
    offset = (lag_ids.astype(jnp.float32) - 0.5 * pulse_len) / pulse_len
    phase_arg = math.pi * pulse_len * range_rate * offset * offset
    amplitude = 1.0 / math.sqrt(pulse_len)
    real_tab = jnp.where(inside, jnp.cos(phase_arg) * amplitude, 0.0).astype(jnp.bfloat16)
    imag_tab = jnp.where(inside, -jnp.sin(phase_arg) * amplitude, 0.0).astype(jnp.bfloat16)
    return (real_tab, imag_tab)

def range_compress(echo_lines, range_rate, product):
    pulse_len = RG // 2
    block_size = min(RG, 256)
    real_tab, imag_tab = chirp_block(range_rate, pulse_len + block_size, block_size)
    line_count = echo_lines.shape[1]
    stacked = echo_lines.reshape(2 * line_count, RG)
    extended = jnp.concatenate([stacked, stacked[:, :pulse_len]], axis=1)

    def one_block(block_id):
        window = lax.dynamic_slice_in_dim(extended, block_id * block_size, pulse_len + block_size, 1)
        with_real = product(window, real_tab)
        with_imag = product(window, imag_tab)
        real_out = with_real[:line_count] - with_imag[line_count:]
        imag_out = with_imag[:line_count] + with_real[line_count:]
        return jnp.stack([real_out, imag_out])
    blocks = lax.map(one_block, jnp.arange(RG // block_size, dtype=jnp.int32))
    return blocks.transpose(1, 2, 0, 3).reshape(2, line_count, RG)

def fourier_rows(first_row, row_count, length):
    row_ids = lax.broadcasted_iota(jnp.int32, (row_count, length), 0) + first_row
    col_ids = lax.broadcasted_iota(jnp.int32, (row_count, length), 1)
    turn_angle = (row_ids * col_ids % length).astype(jnp.float32) * (two_pi / length)
    amplitude = 1.0 / math.sqrt(length)
    return ((jnp.cos(turn_angle) * amplitude).astype(jnp.bfloat16), (-jnp.sin(turn_angle) * amplitude).astype(jnp.bfloat16))

def azimuth_compress(columns, azimuth_rate, product):
    col_count = columns.shape[2]
    joined = jnp.concatenate([columns[0], columns[1]], axis=1)
    block_size = min(AZ, 256)
    block_ids = jnp.arange(AZ // block_size, dtype=jnp.int32)

    def forward_block(block_id):
        first_row = block_id * block_size
        real_tab, imag_tab = fourier_rows(first_row, block_size, AZ)
        with_real = product(real_tab, joined)
        with_imag = product(imag_tab, joined)
        spectrum_re = with_real[:, :col_count] - with_imag[:, col_count:]
        spectrum_im = with_real[:, col_count:] + with_imag[:, :col_count]
        freq_ids = lax.broadcasted_iota(jnp.int32, (block_size, 1), 0) + first_row
        centered = ((freq_ids + AZ // 2) % AZ - AZ // 2).astype(jnp.float32) / AZ
        phase_arg = math.pi * AZ * azimuth_rate[None, :] * centered * centered
        filter_re = jnp.cos(phase_arg)
        filter_im = jnp.sin(phase_arg)
        out_re = spectrum_re * filter_re - spectrum_im * filter_im
        out_im = spectrum_re * filter_im + spectrum_im * filter_re
        return jnp.concatenate([out_re, out_im], axis=1).astype(jnp.bfloat16)
    filtered = lax.map(forward_block, block_ids).reshape(AZ, 2 * col_count)

    def inverse_block(block_id):
        real_tab, imag_tab = fourier_rows(block_id * block_size, block_size, AZ)
        with_real = product(real_tab, filtered)
        with_imag = product(imag_tab, filtered)
        focus_re = with_real[:, :col_count] + with_imag[:, col_count:]
        focus_im = with_real[:, col_count:] - with_imag[:, :col_count]
        return jnp.stack([focus_re, focus_im]).astype(jnp.bfloat16)
    pieces = lax.map(inverse_block, block_ids)
    return pieces.transpose(1, 0, 2, 3).reshape(2, AZ, col_count)

def kernel_taps(fraction):
    half_taps = TAPS // 2
    position = jnp.arange(TAPS, dtype=jnp.int32).astype(jnp.float32) - (half_taps - 1) - fraction
    return jnp.sinc(position) * (0.5 + 0.5 * jnp.cos(math.pi * position / half_taps))

def interpolate(window, tap_weights, out_rows):
    running = tap_weights[0] * window[:, 0:out_rows].astype(jnp.float32)
    for tap_id in range(1, TAPS):
        running = running + tap_weights[tap_id] * window[:, tap_id:tap_id + out_rows].astype(jnp.float32)
    return running.astype(jnp.bfloat16)

def own_power(block_data):
    as_float = block_data.astype(jnp.float32)
    return as_float[0] * as_float[0] + as_float[1] * as_float[1]

def pair_terms(own_block, other_block):
    own_f = own_block.astype(jnp.float32)
    other_f = other_block.astype(jnp.float32)
    cross_re = own_f[0] * other_f[0] + own_f[1] * other_f[1]
    cross_im = own_f[1] * other_f[0] - own_f[0] * other_f[1]
    power_b = other_f[0] * other_f[0] + other_f[1] * other_f[1]
    return jnp.stack([cross_re, cross_im, power_b])

def box_sum(values, out_rows):
    half_rg = WIN_RG // 2
    padded = jnp.pad(values, ((0, 0), (0, 0), (half_rg, half_rg)))
    sample_count = values.shape[2]
    across = padded[:, :, 0:sample_count]
    for offset_id in range(1, WIN_RG):
        across = across + padded[:, :, offset_id:offset_id + sample_count]
    running = across[:, 0:out_rows]
    for offset_id in range(1, WIN_AZ):
        running = running + across[:, offset_id:offset_id + out_rows]
    return running

def coherence_of(box_terms, power_box):
    denominator = jnp.sqrt(power_box * box_terms[2] + epsilon)
    return jnp.stack([box_terms[0] / denominator, box_terms[1] / denominator]).astype(jnp.bfloat16)

def reference(raw_echo, range_rate, azimuth_rate, line_offset, frac_shift):
    rim_lines = MAX_OFF + TAPS - 1

    def focus_date(date_id):
        compressed = range_compress(raw_echo[date_id], range_rate, exact_dot).astype(jnp.bfloat16)
        focused = azimuth_compress(compressed, azimuth_rate, exact_dot)
        extended = jnp.concatenate([focused, focused[:, :rim_lines]], axis=1)
        window = lax.dynamic_slice_in_dim(extended, line_offset[date_id].astype(jnp.int32), AZ + TAPS - 1, 1)
        return interpolate(window, kernel_taps(frac_shift[date_id]), AZ)
    date_ids = jnp.arange(DATES, dtype=jnp.int32)
    coregistered = lax.map(focus_date, date_ids)
    half_win = WIN_AZ // 2
    bordered = jnp.pad(coregistered, ((0, 0), (0, 0), (half_win, half_win), (0, 0)))

    def pair_date(date_id):
        own_block = bordered[date_id]
        power_box = box_sum(own_power(own_block)[None], AZ)[0]
        results = []
        for step_id in range(SPAN):
            partner = bordered[(date_id + step_id + 1) % DATES]
            results.append(coherence_of(box_sum(pair_terms(own_block, partner), AZ), power_box))
        return jnp.stack(results)
    coherence = lax.map(pair_date, date_ids)
    return (coregistered, coherence)
```

```python
import functools
import math

import jax
import jax.numpy as jnp
from jax import lax
from jax.experimental import pallas as pl
from jax.experimental.pallas import tpu as pltpu
from jax.sharding import PartitionSpec as P

TAPS = 8
WIN_AZ = 11
WIN_RG = 5
SPAN = 2
LANES = 128
PACK = 16
RIM = 8
LINE_STEP = 64

two_pi = 2.0 * math.pi
epsilon = 1e-06
F32 = jnp.float32
BF16 = jnp.bfloat16


def params(mib):
    return pltpu.CompilerParams(vmem_limit_bytes=mib * 1024 * 1024)


def cost(flops, bytes_accessed):
    return pl.CostEstimate(flops=int(flops), bytes_accessed=int(bytes_accessed), transcendentals=0)


def vmem():
    return pl.BlockSpec(memory_space=pltpu.VMEM)


def smem():
    return pl.BlockSpec(memory_space=pltpu.SMEM)


def sincos_turns(turns):
    quarter = jnp.floor(turns * 4.0 + 0.5)
    x = (turns - quarter * 0.25) * two_pi
    x2 = x * x
    s = x * (1.0 + x2 * (-1.0 / 6 + x2 * (1.0 / 120 + x2 * (-1.0 / 5040 + x2 * (1.0 / 362880)))))
    c = 1.0 + x2 * (-0.5 + x2 * (1.0 / 24 + x2 * (-1.0 / 720 + x2 * (1.0 / 40320))))
    quad = quarter.astype(jnp.int32) & 3
    odd = (quad & 1) == 1
    sin_v = jnp.where(odd, c, s)
    cos_v = jnp.where(odd, s, c)
    sin_v = jnp.where(quad >= 2, -sin_v, sin_v)
    cos_v = jnp.where((quad == 1) | (quad == 2), -cos_v, cos_v)
    return sin_v, cos_v


def build_chirp(rate_ref, table_ref, base_ref, pulse_len, width):
    top = pulse_len + width - PACK
    span = base_ref.shape[2]
    lag = (
        lax.broadcasted_iota(jnp.int32, (PACK, span), 0)
        + top
        - lax.broadcasted_iota(jnp.int32, (PACK, span), 1)
    )
    inside = (lag >= 0) & (lag < pulse_len)
    offset = (lag.astype(F32) - 0.5 * pulse_len) / pulse_len
    turns = 0.5 * pulse_len * rate_ref[0] * offset * offset
    sin_v, cos_v = sincos_turns(turns)
    amplitude = 1.0 / math.sqrt(pulse_len)
    base_ref[0] = jnp.where(inside, cos_v * amplitude, 0.0)
    base_ref[1] = jnp.where(inside, -sin_v * amplitude, 0.0)
    for block in range((pulse_len + width) // PACK):
        start = top - PACK * block
        aligned = start // LANES * LANES
        skew = start - aligned
        size = width + LANES
        for part in range(2):
            window = base_ref[part, :, aligned : aligned + size]
            if skew:
                window = pltpu.roll(window, size - skew, 1)
            table_ref[block * PACK : (block + 1) * PACK, part * width : (part + 1) * width] = (
                window[:, :width].astype(BF16)
            )


def range_blocks(me_ref, echo_ref, table, outs, chunks, chunk_count, devices, pulse_len):
    lines = echo_ref.shape[0] // 2
    samples = echo_ref.shape[1]
    width = outs[0].shape[1] // 2
    lane_blocks = samples // LANES
    window_blocks = (pulse_len + width) // LANES
    index = 0
    for chunk in chunks:
        for step in range(devices):
            target = lax.rem(me_ref[0] + step, devices)
            first = target * (samples // devices // LANES) + chunk * (width // LANES)
            pieces = [
                echo_ref[
                    :,
                    pl.ds(
                        pl.multiple_of(lax.rem(first + j, lane_blocks) * LANES, LANES), LANES
                    ),
                ]
                for j in range(window_blocks)
            ]
            window = jnp.concatenate(pieces, axis=1)
            product = jnp.dot(window, table, preferred_element_type=F32)
            out = outs[index]
            out[:, :width] = (product[:lines, :width] - product[lines:, width:]).astype(BF16)
            out[:, width:] = (product[lines:, :width] + product[:lines, width:]).astype(BF16)
            index += 1


def first_range_kernel(devices, chunk_count, pulse_len, me_ref, rate_ref, echo_ref, table_ref, *rest):
    outs, base_ref = rest[:-1], rest[-1]
    width = table_ref.shape[1] // 2
    build_chirp(rate_ref, table_ref, base_ref, pulse_len, width)
    range_blocks(
        me_ref, echo_ref, table_ref[...], outs, [0], chunk_count, devices, pulse_len
    )


def rest_range_kernel(devices, chunk_count, pulse_len, me_ref, echo_ref, table_ref, *outs):
    range_blocks(
        me_ref,
        echo_ref,
        table_ref[...],
        outs,
        range(1, chunk_count),
        chunk_count,
        devices,
        pulse_len,
    )


def tables_kernel(
    shift_ref, taps_ref, rate_ref, _, dft_ref, inv_ref, coef_ref, filt_ref
):
    size = dft_ref.shape[0]
    half = size // 2
    amplitude = 1.0 / math.sqrt(size)
    rows = lax.broadcasted_iota(jnp.int32, (PACK, LANES), 0)
    lanes = lax.broadcasted_iota(jnp.int32, (PACK, LANES), 1)
    period = size // LANES
    turn_of = []
    for block in range(period):
        sin_b, cos_b = sincos_turns(((rows * block) % period).astype(F32) / period)
        turn_of.append((sin_b * amplitude, cos_b * amplitude))

    def base_of(ids):
        return sincos_turns(((ids * lanes) & (size - 1)).astype(F32) / size)

    def alternate(ids):
        return jnp.where((ids & 1) == 0, amplitude, -amplitude)

    def dft_rows(tile, _):
        ids = rows + tile * PACK
        sin_0, cos_0 = base_of(ids)
        row = pl.multiple_of(tile * PACK, PACK)
        for block in range(period):
            sin_b, cos_b = turn_of[block]
            cols = slice(block * LANES, (block + 1) * LANES)
            dft_ref[pl.ds(row, PACK), cols] = (cos_0 * cos_b - sin_0 * sin_b).astype(BF16)
            sin_v = sin_0 * cos_b + cos_0 * sin_b
            sin_v = jnp.where(ids == 0, alternate(lanes), sin_v)
            dft_ref[pl.ds(half + row, PACK), cols] = sin_v.astype(BF16)
        return 0

    lax.fori_loop(0, half // PACK, dft_rows, 0)

    def inv_rows(tile, _):
        ids = rows + (tile * PACK - RIM)
        sin_0, cos_0 = base_of(ids)
        row = pl.multiple_of(tile * PACK, PACK)
        for block in range(half // LANES):
            sin_b, cos_b = turn_of[block]
            cos_v = cos_0 * cos_b - sin_0 * sin_b
            sin_v = sin_0 * cos_b + cos_0 * sin_b
            if block == 0:
                sin_v = jnp.where(lanes == 0, alternate(ids), sin_v)
            first = block * LANES
            inv_ref[pl.ds(row, PACK), first : first + LANES] = cos_v.astype(BF16)
            first += half
            inv_ref[pl.ds(row, PACK), first : first + LANES] = sin_v.astype(BF16)
        return 0

    lax.fori_loop(0, inv_ref.shape[0] // PACK, inv_rows, 0)

    shift = shift_ref[0]

    def coef_rows(tile, _):
        ids = rows + tile * PACK
        row = pl.multiple_of(tile * PACK, PACK)
        sin_v, cos_v = sincos_turns(((ids * shift) & (size - 1)).astype(F32) / size)
        sin_1, cos_1 = sincos_turns(ids.astype(F32) / size)
        sum_c = taps_ref[0] * cos_v
        sum_s = taps_ref[0] * sin_v
        for tap in range(1, TAPS):
            sin_v, cos_v = sin_v * cos_1 + cos_v * sin_1, cos_v * cos_1 - sin_v * sin_1
            sum_c = sum_c + taps_ref[tap] * cos_v
            sum_s = sum_s + taps_ref[tap] * sin_v
        first = ids == 0
        coef_ref[0, pl.ds(row, PACK), :] = jnp.where(first, sum_c, 2.0 * sum_c)
        coef_ref[1, pl.ds(row, PACK), :] = 2.0 * sum_s
        coef_ref[2, pl.ds(row, PACK), :] = jnp.where(first, taps_ref[TAPS], 2.0 * sum_c)
        return 0

    lax.fori_loop(0, half // PACK, coef_rows, 0)

    width = rate_ref.shape[1]
    rate = rate_ref[...]

    def filter_rows(tile, _):
        ids = lax.broadcasted_iota(jnp.int32, (RIM, width), 0) + tile * RIM
        row = pl.multiple_of(tile * RIM, RIM)
        centered = jnp.minimum(ids, half).astype(F32) / size
        sin_v, cos_v = sincos_turns(0.5 * size * rate * centered * centered)
        filt_ref[0, pl.ds(row, RIM), :] = cos_v
        filt_ref[1, pl.ds(row, RIM), :] = sin_v
        return 0

    lax.fori_loop(0, half // RIM + 1, filter_rows, 0)


def forward_kernel(devices, chunk, me_ref, dft_ref, coef_ref, filt_ref, *rest):
    blocks, out_ref, joined = rest[:devices], rest[devices], rest[devices + 1]
    size = dft_ref.shape[0]
    half = size // 2
    lines, width = blocks[0].shape[0], blocks[0].shape[1] // 2
    for step in range(devices):
        source = lax.rem(me_ref[0] + (devices - step), devices)
        joined[pl.ds(pl.multiple_of(source * lines, lines), lines), :] = blocks[step][...]
    columns = joined[...]
    tile = min(half, 128)
    copies = width // LANES
    for first in range(0, half, tile):
        rows = slice(first, first + tile)
        even = jnp.dot(dft_ref[rows, :], columns, preferred_element_type=F32)
        odd = jnp.dot(
            dft_ref[half + first : half + first + tile, :], columns, preferred_element_type=F32
        )
        coefs = [coef_ref[i, rows, :] for i in range(3)]
        if copies > 1:
            coefs = [jnp.concatenate([value] * copies, axis=1) for value in coefs]
        even_re, even_im = even[:, :width], even[:, width:]
        odd_re, odd_im = odd[:, :width], odd[:, width:]
        u_re = coefs[0] * even_re + coefs[1] * odd_re
        u_im = coefs[0] * even_im + coefs[1] * odd_im
        v_re = coefs[2] * odd_re - coefs[1] * even_re
        v_im = coefs[2] * odd_im - coefs[1] * even_im
        cols = slice(chunk * width, (chunk + 1) * width)
        filt_re, filt_im = filt_ref[0, rows, cols], filt_ref[1, rows, cols]
        out_ref[rows, :width] = (filt_re * u_re - filt_im * u_im).astype(BF16)
        out_ref[rows, width:] = (filt_re * u_im + filt_im * u_re).astype(BF16)
        if first == 0:
            top = lax.broadcasted_iota(jnp.int32, (tile, width), 0) == 0
            filt_re = jnp.where(top, filt_ref[0, half : half + 1, cols], filt_re)
            filt_im = jnp.where(top, filt_ref[1, half : half + 1, cols], filt_im)
        rows = slice(half + first, half + first + tile)
        out_ref[rows, :width] = (filt_re * v_re - filt_im * v_im).astype(BF16)
        out_ref[rows, width:] = (filt_re * v_im + filt_im * v_re).astype(BF16)


def inverse_kernel(devices, line_count, first_row, rows, chunk_count, me_ref, inv_ref, *rest):
    spectra, outs = rest[:chunk_count], rest[chunk_count:]
    pieces = []
    for step in range(devices):
        target = lax.rem(me_ref[0] + step, devices)
        start = pl.multiple_of(target * line_count + first_row, PACK)
        pieces.append(inv_ref[pl.ds(start, rows), :])
    left = jnp.concatenate(pieces, axis=0)
    total = outs[0].shape[1] // 2
    width = total // chunk_count
    for chunk in range(chunk_count):
        product = jnp.dot(left, spectra[chunk][...], preferred_element_type=F32).astype(BF16)
        for step in range(devices):
            part = product[step * rows : (step + 1) * rows]
            first = chunk * width
            outs[step][:, first : first + width] = part[:, :width]
            first += total
            outs[step][:, first : first + width] = part[:, width:]


def join_kernel(devices, has_first, has_last, me_ref, *rest):
    blocks, out_ref = rest[:devices], rest[devices]
    rows, width = blocks[0].shape[0], blocks[0].shape[1] // 2
    samples = out_ref.shape[1] // 2
    for step in range(devices):
        source = lax.rem(me_ref[0] + (devices - step), devices)
        for part in range(2):
            start = pl.multiple_of(part * samples + source * width, LANES)
            out_ref[:, pl.ds(start, width)] = blocks[step][:, part * width : (part + 1) * width]

    def clear(first, low, high):
        edge = out_ref[first : first + PACK, :].astype(F32)
        ids = lax.broadcasted_iota(jnp.int32, edge.shape, 0)
        edge = jnp.where((ids >= low) & (ids < high), 0.0, edge)
        out_ref[first : first + PACK, :] = edge.astype(BF16)

    if has_first:

        @pl.when(me_ref[0] == 0)
        def _():
            clear(0, 0, RIM)

    if has_last:

        @pl.when(me_ref[0] == devices - 1)
        def _():
            clear(rows - PACK, PACK - RIM, PACK)


def coherence_kernel(has_before, *refs):
    dates = SPAN + 1
    now = refs[:dates]
    position = dates
    before = None
    if has_before:
        before = refs[position : position + dates]
        position += dates + 2
    image_ref, result_ref, sums_ref = refs[position : position + 3]
    lines = image_ref.shape[1]
    samples = image_ref.shape[2]
    window = lines + 2 * RIM
    half_az, half_rg = WIN_AZ // 2, WIN_RG // 2
    block = min(samples, 256)
    out_id = lax.broadcasted_iota(jnp.int32, (lines, window), 0)
    in_id = lax.broadcasted_iota(jnp.int32, (lines, window), 1) - RIM
    band = jnp.where(jnp.abs(in_id - out_id) <= half_az, 1.0, 0.0).astype(BF16)
    band = jnp.concatenate([band, band], axis=1)
    terms = 1 + 3 * SPAN

    def load(date, start):
        piece = now[date][:, pl.ds(start, block)]
        if has_before:
            held = before[date]
            piece = jnp.concatenate(
                [held[held.shape[0] - 2 * RIM :, pl.ds(start, block)], piece], axis=0
            )
        return piece

    def add_lines(value, term, start):
        high = value.astype(BF16)
        low = (value - high.astype(F32)).astype(BF16)
        both = jnp.concatenate([high, low], axis=0)
        sums_ref[term, :, pl.ds(start + LANES, block)] = jnp.dot(
            band, both, preferred_element_type=F32
        )

    def first_pass(index, _):
        start = pl.multiple_of(index * block, block)
        re = load(0, start)
        im = load(0, samples + start)
        re, im = re.astype(F32), im.astype(F32)
        image_ref[0, :, pl.ds(start, block)] = re[RIM : RIM + lines].astype(BF16)
        image_ref[1, :, pl.ds(start, block)] = im[RIM : RIM + lines].astype(BF16)
        add_lines(re * re + im * im, 0, start)
        for date in range(1, dates):
            other_re = load(date, start).astype(F32)
            other_im = load(date, samples + start).astype(F32)
            term = 3 * date - 2
            add_lines(re * other_re + im * other_im, term, start)
            add_lines(im * other_re - re * other_im, term + 1, start)
            add_lines(other_re * other_re + other_im * other_im, term + 2, start)
        return 0

    edge = jnp.zeros((lines, LANES), F32)
    for term in range(terms):
        sums_ref[term, :, :LANES] = edge
        sums_ref[term, :, samples + LANES :] = edge
    lax.fori_loop(0, samples // block, first_pass, 0)

    def second_pass(index, _):
        start = pl.multiple_of(index * block, block)
        size = block + 2 * LANES

        def box(term):
            wide = sums_ref[term, :, pl.ds(start, size)]
            pair = wide + pltpu.roll(wide, 1, 1)
            four = pair + pltpu.roll(pair, 2, 1)
            five = four + pltpu.roll(wide, 4, 1)
            return pltpu.roll(five, size - half_rg, 1)[:, LANES : LANES + block]

        own = box(0)
        for date in range(1, dates):
            term = 3 * date - 2
            scale = lax.rsqrt(own * box(term + 2) + epsilon)
            result_ref[date - 1, 0, :, pl.ds(start, block)] = (box(term) * scale).astype(BF16)
            result_ref[date - 1, 1, :, pl.ds(start, block)] = (box(term + 1) * scale).astype(BF16)
        return 0

    lax.fori_loop(0, samples // block, second_pass, 0)


def kernel_taps(fraction):
    half_taps = TAPS // 2
    position = jnp.arange(TAPS, dtype=jnp.int32).astype(F32) - (half_taps - 1) - fraction
    return jnp.sinc(position) * (0.5 + 0.5 * jnp.cos(math.pi * position / half_taps))


def scatter(blocks, axis):
    count = lax.axis_size(axis)
    moved = [blocks[0]]
    for step in range(1, count):
        route = [(i, (i + step) % count) for i in range(count)]
        moved.append(lax.ppermute(blocks[step], axis, route))
    return moved


def from_next(block, axis):
    count = lax.axis_size(axis)
    return lax.ppermute(block, axis, [((i + 1) % count, i) for i in range(count)])


def body(raw_echo, range_rate, azimuth_rate, line_offset, frac_shift):
    devices = lax.axis_size("swath")
    lines, samples = raw_echo.shape[2], raw_echo.shape[3]
    size = lines * devices
    half = size // 2
    owned = azimuth_rate.shape[0]
    pulse_len = samples // 2
    me = lax.axis_index("swath").astype(jnp.int32).reshape(1)
    echo = raw_echo.reshape(2 * lines, samples)

    chunk_count = max(1, min(4, owned // LANES))
    width = owned // chunk_count
    depth = pulse_len + width
    block_type = jax.ShapeDtypeStruct((lines, 2 * width), BF16)
    flops = 2 * 2 * lines * depth * 2 * width * devices
    table, *first_blocks = pl.pallas_call(
        functools.partial(first_range_kernel, devices, chunk_count, pulse_len),
        out_shape=[jax.ShapeDtypeStruct((depth, 2 * width), BF16)] + [block_type] * devices,
        in_specs=[smem(), smem(), vmem()],
        out_specs=[vmem()] * (devices + 1),
        scratch_shapes=[pltpu.VMEM((2, PACK, pulse_len + 2 * width + LANES), F32)],
        compiler_params=params(40),
        cost_estimate=cost(2 * flops, 4 * lines * samples),
        name="range_first",
    )(me, range_rate.reshape(1), echo)
    columns = [scatter(first_blocks, "swath")]
    order = first_blocks[0]
    if chunk_count > 1:
        rest = pl.pallas_call(
            functools.partial(rest_range_kernel, devices, chunk_count, pulse_len),
            out_shape=[block_type] * (devices * (chunk_count - 1)),
            in_specs=[smem(), vmem(), vmem()],
            out_specs=[vmem()] * (devices * (chunk_count - 1)),
            compiler_params=params(40),
            cost_estimate=cost((chunk_count - 1) * flops, 4 * lines * samples),
            name="range_rest",
        )(me, echo, table)
        for chunk in range(chunk_count - 1):
            columns.append(scatter(rest[chunk * devices : (chunk + 1) * devices], "swath"))
        order = rest[-1]

    taps = kernel_taps(frac_shift[0])
    signs = 1.0 - 2.0 * ((line_offset[0] + jnp.arange(TAPS, dtype=jnp.int32)) % 2).astype(F32)
    taps = jnp.concatenate([taps, jnp.sum(taps * signs).reshape(1)])
    dft, inv, coef, filt = pl.pallas_call(
        tables_kernel,
        out_shape=[
            jax.ShapeDtypeStruct((size, size), BF16),
            jax.ShapeDtypeStruct((size + 2 * RIM, size), BF16),
            jax.ShapeDtypeStruct((3, half, LANES), F32),
            jax.ShapeDtypeStruct((2, half + RIM, owned), F32),
        ],
        in_specs=[smem(), smem(), vmem(), pl.BlockSpec(memory_space=pl.ANY)],
        out_specs=[vmem()] * 4,
        compiler_params=params(40),
        cost_estimate=cost(size * size * 64, 8 * size * size),
        name="azimuth_tables",
    )(line_offset, taps, azimuth_rate.reshape(1, owned), order)

    spectra = []
    for chunk in range(chunk_count):
        spectra.append(
            pl.pallas_call(
                functools.partial(forward_kernel, devices, chunk),
                out_shape=jax.ShapeDtypeStruct((size, 2 * width), BF16),
                in_specs=[smem()] + [vmem()] * (3 + devices),
                out_specs=vmem(),
                scratch_shapes=[pltpu.VMEM((size, 2 * width), BF16)],
                compiler_params=params(40),
                cost_estimate=cost(4 * size * size * width, 2 * size * size + 8 * size * width),
                name="azimuth_forward",
            )(me, dft, coef, filt, *columns[chunk])
        )

    step_lines = min(lines, LINE_STEP)
    steps = lines // step_lines
    image = result = held = None
    for step in range(steps):
        rows = step_lines + (2 * RIM if step == 0 else 0)
        first_row = step * step_lines + (0 if step == 0 else 2 * RIM)
        outs = pl.pallas_call(
            functools.partial(inverse_kernel, devices, lines, first_row, rows, chunk_count),
            out_shape=[jax.ShapeDtypeStruct((rows, 2 * owned), BF16)] * devices,
            in_specs=[smem()] + [vmem()] * (1 + chunk_count),
            out_specs=[vmem()] * devices,
            compiler_params=params(40),
            cost_estimate=cost(
                4 * devices * rows * size * owned, 2 * size * size + 4 * size * owned
            ),
            name="azimuth_inverse",
        )(me, inv, *spectra)
        strips = scatter(outs, "swath")
        own = pl.pallas_call(
            functools.partial(join_kernel, devices, step == 0, step == steps - 1),
            out_shape=jax.ShapeDtypeStruct((rows, 2 * samples), BF16),
            in_specs=[smem()] + [vmem()] * devices,
            out_specs=vmem(),
            compiler_params=params(40),
            cost_estimate=cost(rows * samples, 8 * rows * samples),
            name="join_strips",
        )(me, *strips)
        now = [own]
        for _ in range(SPAN):
            now.append(from_next(now[-1], "date"))
        operands = list(now)
        in_specs = [vmem()] * len(now)
        aliases = {}
        if held is not None:
            operands += held + [image, result]
            in_specs += [vmem()] * len(held) + [pl.BlockSpec(memory_space=pl.ANY)] * 2
            aliases = {len(operands) - 2: 0, len(operands) - 1: 1}
        image, result = pl.pallas_call(
            functools.partial(coherence_kernel, held is not None),
            grid=(1,),
            out_shape=[
                jax.ShapeDtypeStruct((2, lines, samples), BF16),
                jax.ShapeDtypeStruct((SPAN, 2, lines, samples), BF16),
            ],
            in_specs=in_specs,
            out_specs=[
                pl.BlockSpec((2, step_lines, samples), lambda i, s=step: (0, s, 0)),
                pl.BlockSpec((SPAN, 2, step_lines, samples), lambda i, s=step: (0, 0, s, 0)),
            ],
            scratch_shapes=[
                pltpu.VMEM((1 + 3 * SPAN, step_lines, samples + 2 * LANES), F32)
            ],
            input_output_aliases=aliases,
            compiler_params=params(48),
            cost_estimate=cost(500 * step_lines * samples, 30 * step_lines * samples),
            name="coherence",
        )(*operands)
        held = now
    return (image[None], result[None])


def solution(mesh):
    placed = (P("date", None, "swath", None), P(), P("swath"), P("date"), P("date"))
    return jax.shard_map(
        body,
        mesh=mesh,
        in_specs=placed,
        out_specs=(P("date", None, "swath", None), P("date", None, None, "swath", None)),
        check_vma=False,
    )
```

```python
import functools
import math

import jax
import jax.numpy as jnp
from jax import lax
from jax.experimental import pallas as pl
from jax.experimental.pallas import tpu as pltpu
from jax.sharding import PartitionSpec as P

TAPS = 8
WIN_AZ = 11
WIN_RG = 5
SPAN = 2
LANES = 128
PACK = 16
RIM = 8
LINE_STEP = 64

two_pi = 2.0 * math.pi
epsilon = 1e-06
F32 = jnp.float32
BF16 = jnp.bfloat16


def params(mib):
    return pltpu.CompilerParams(vmem_limit_bytes=mib * 1024 * 1024)


def cost(micros):
    return pl.CostEstimate(flops=int(micros * 1e9), bytes_accessed=0, transcendentals=0)


def vmem():
    return pl.BlockSpec(memory_space=pltpu.VMEM)


def hold():
    return pl.BlockSpec(memory_space=pl.ANY)


def smem():
    return pl.BlockSpec(memory_space=pltpu.SMEM)


def sincos_turns(turns):
    quarter = jnp.floor(turns * 4.0 + 0.5)
    x = (turns - quarter * 0.25) * two_pi
    x2 = x * x
    s = x * (1.0 + x2 * (-1.0 / 6 + x2 * (1.0 / 120 + x2 * (-1.0 / 5040 + x2 * (1.0 / 362880)))))
    c = 1.0 + x2 * (-0.5 + x2 * (1.0 / 24 + x2 * (-1.0 / 720 + x2 * (1.0 / 40320))))
    quad = quarter.astype(jnp.int32) & 3
    odd = (quad & 1) == 1
    sin_v = jnp.where(odd, c, s)
    cos_v = jnp.where(odd, s, c)
    sin_v = jnp.where(quad >= 2, -sin_v, sin_v)
    cos_v = jnp.where((quad == 1) | (quad == 2), -cos_v, cos_v)
    return sin_v, cos_v


def build_chirp(rate_ref, table_ref, base_ref, pulse_len, width):
    top = pulse_len + width - PACK
    span = base_ref.shape[2]
    lag = (
        lax.broadcasted_iota(jnp.int32, (PACK, span), 0)
        + top
        - lax.broadcasted_iota(jnp.int32, (PACK, span), 1)
    )
    inside = (lag >= 0) & (lag < pulse_len)
    offset = (lag.astype(F32) - 0.5 * pulse_len) / pulse_len
    turns = 0.5 * pulse_len * rate_ref[0] * offset * offset
    sin_v, cos_v = sincos_turns(turns)
    amplitude = 1.0 / math.sqrt(pulse_len)
    base_ref[0] = jnp.where(inside, cos_v * amplitude, 0.0)
    base_ref[1] = jnp.where(inside, -sin_v * amplitude, 0.0)
    for block in range((pulse_len + width) // PACK):
        start = top - PACK * block
        aligned = start // LANES * LANES
        skew = start - aligned
        size = width + LANES
        for part in range(2):
            window = base_ref[part, :, aligned : aligned + size]
            if skew:
                window = pltpu.roll(window, size - skew, 1)
            table_ref[block * PACK : (block + 1) * PACK, part * width : (part + 1) * width] = (
                window[:, :width].astype(BF16)
            )


def range_blocks(me_ref, echo_ref, table, outs, chunk, devices, pulse_len):
    lines = echo_ref.shape[0] // 2
    samples = echo_ref.shape[1]
    width = outs[0].shape[1] // 2
    lane_blocks = samples // LANES
    window_blocks = (pulse_len + width) // LANES
    for step in range(devices):
        target = lax.rem(me_ref[0] + step, devices)
        first = target * (samples // devices // LANES) + chunk * (width // LANES)
        pieces = [
            echo_ref[
                :,
                pl.ds(pl.multiple_of(lax.rem(first + j, lane_blocks) * LANES, LANES), LANES),
            ]
            for j in range(window_blocks)
        ]
        window = jnp.concatenate(pieces, axis=1)
        product = jnp.dot(window, table, preferred_element_type=F32)
        out = outs[step]
        out[:, :width] = (product[:lines, :width] - product[lines:, width:]).astype(BF16)
        out[:, width:] = (product[lines:, :width] + product[:lines, width:]).astype(BF16)


def first_range_kernel(devices, pulse_len, me_ref, rate_ref, echo_ref, table_ref, *rest):
    outs, base_ref = rest[:-1], rest[-1]
    width = table_ref.shape[1] // 2
    build_chirp(rate_ref, table_ref, base_ref, pulse_len, width)
    range_blocks(me_ref, echo_ref, table_ref[...], outs, 0, devices, pulse_len)


def next_range_kernel(devices, chunk, pulse_len, me_ref, echo_ref, table_ref, _, *outs):
    range_blocks(me_ref, echo_ref, table_ref[...], outs, chunk, devices, pulse_len)


def tables_kernel(
    shift_ref, taps_ref, rate_ref, _, dft_ref, inv_ref, coef_ref, filt_ref
):
    size = dft_ref.shape[0]
    half = size // 2
    amplitude = 1.0 / math.sqrt(size)
    rows = lax.broadcasted_iota(jnp.int32, (PACK, LANES), 0)
    lanes = lax.broadcasted_iota(jnp.int32, (PACK, LANES), 1)
    period = size // LANES
    turn_of = []
    for block in range(period):
        sin_b, cos_b = sincos_turns(((rows * block) % period).astype(F32) / period)
        turn_of.append((sin_b * amplitude, cos_b * amplitude))

    def base_of(ids):
        return sincos_turns(((ids * lanes) & (size - 1)).astype(F32) / size)

    def alternate(ids):
        return jnp.where((ids & 1) == 0, amplitude, -amplitude)

    def dft_rows(tile, _):
        ids = rows + tile * PACK
        sin_0, cos_0 = base_of(ids)
        row = pl.multiple_of(tile * PACK, PACK)
        for block in range(period):
            sin_b, cos_b = turn_of[block]
            cols = slice(block * LANES, (block + 1) * LANES)
            dft_ref[pl.ds(row, PACK), cols] = (cos_0 * cos_b - sin_0 * sin_b).astype(BF16)
            sin_v = sin_0 * cos_b + cos_0 * sin_b
            sin_v = jnp.where(ids == 0, alternate(lanes), sin_v)
            dft_ref[pl.ds(half + row, PACK), cols] = sin_v.astype(BF16)
        return 0

    lax.fori_loop(0, half // PACK, dft_rows, 0)

    def inv_rows(tile, _):
        ids = rows + (tile * PACK - RIM)
        sin_0, cos_0 = base_of(ids)
        row = pl.multiple_of(tile * PACK, PACK)
        for block in range(half // LANES):
            sin_b, cos_b = turn_of[block]
            cos_v = cos_0 * cos_b - sin_0 * sin_b
            sin_v = sin_0 * cos_b + cos_0 * sin_b
            if block == 0:
                sin_v = jnp.where(lanes == 0, alternate(ids), sin_v)
            first = block * LANES
            inv_ref[pl.ds(row, PACK), first : first + LANES] = cos_v.astype(BF16)
            first += half
            inv_ref[pl.ds(row, PACK), first : first + LANES] = sin_v.astype(BF16)
        return 0

    lax.fori_loop(0, inv_ref.shape[0] // PACK, inv_rows, 0)

    shift = shift_ref[0]

    def coef_rows(tile, _):
        ids = rows + tile * PACK
        row = pl.multiple_of(tile * PACK, PACK)
        sin_v, cos_v = sincos_turns(((ids * shift) & (size - 1)).astype(F32) / size)
        sin_1, cos_1 = sincos_turns(ids.astype(F32) / size)
        sum_c = taps_ref[0] * cos_v
        sum_s = taps_ref[0] * sin_v
        for tap in range(1, TAPS):
            sin_v, cos_v = sin_v * cos_1 + cos_v * sin_1, cos_v * cos_1 - sin_v * sin_1
            sum_c = sum_c + taps_ref[tap] * cos_v
            sum_s = sum_s + taps_ref[tap] * sin_v
        first = ids == 0
        coef_ref[0, pl.ds(row, PACK), :] = jnp.where(first, sum_c, 2.0 * sum_c)
        coef_ref[1, pl.ds(row, PACK), :] = 2.0 * sum_s
        coef_ref[2, pl.ds(row, PACK), :] = jnp.where(first, taps_ref[TAPS], 2.0 * sum_c)
        return 0

    lax.fori_loop(0, half // PACK, coef_rows, 0)

    width = rate_ref.shape[1]
    rate = rate_ref[...]

    def filter_rows(tile, _):
        ids = lax.broadcasted_iota(jnp.int32, (RIM, width), 0) + tile * RIM
        row = pl.multiple_of(tile * RIM, RIM)
        centered = jnp.minimum(ids, half).astype(F32) / size
        sin_v, cos_v = sincos_turns(0.5 * size * rate * centered * centered)
        filt_ref[0, pl.ds(row, RIM), :] = cos_v
        filt_ref[1, pl.ds(row, RIM), :] = sin_v
        return 0

    lax.fori_loop(0, half // RIM + 1, filter_rows, 0)


def forward_kernel(devices, chunk, me_ref, dft_ref, coef_ref, filt_ref, _, *rest):
    blocks, out_ref, joined = rest[:devices], rest[devices], rest[devices + 1]
    size = dft_ref.shape[0]
    half = size // 2
    lines, width = blocks[0].shape[0], blocks[0].shape[1] // 2
    for step in range(devices):
        source = lax.rem(me_ref[0] + (devices - step), devices)
        joined[pl.ds(pl.multiple_of(source * lines, lines), lines), :] = blocks[step][...]
    columns = joined[...]
    tile = min(half, 128)
    copies = width // LANES
    for first in range(0, half, tile):
        rows = slice(first, first + tile)
        even = jnp.dot(dft_ref[rows, :], columns, preferred_element_type=F32)
        odd = jnp.dot(
            dft_ref[half + first : half + first + tile, :], columns, preferred_element_type=F32
        )
        coefs = [coef_ref[i, rows, :] for i in range(3)]
        if copies > 1:
            coefs = [jnp.concatenate([value] * copies, axis=1) for value in coefs]
        even_re, even_im = even[:, :width], even[:, width:]
        odd_re, odd_im = odd[:, :width], odd[:, width:]
        u_re = coefs[0] * even_re + coefs[1] * odd_re
        u_im = coefs[0] * even_im + coefs[1] * odd_im
        v_re = coefs[2] * odd_re - coefs[1] * even_re
        v_im = coefs[2] * odd_im - coefs[1] * even_im
        cols = slice(chunk * width, (chunk + 1) * width)
        filt_re, filt_im = filt_ref[0, rows, cols], filt_ref[1, rows, cols]
        out_ref[rows, :width] = (filt_re * u_re - filt_im * u_im).astype(BF16)
        out_ref[rows, width:] = (filt_re * u_im + filt_im * u_re).astype(BF16)
        if first == 0:
            top = lax.broadcasted_iota(jnp.int32, (tile, width), 0) == 0
            filt_re = jnp.where(top, filt_ref[0, half : half + 1, cols], filt_re)
            filt_im = jnp.where(top, filt_ref[1, half : half + 1, cols], filt_im)
        rows = slice(half + first, half + first + tile)
        out_ref[rows, :width] = (filt_re * v_re - filt_im * v_im).astype(BF16)
        out_ref[rows, width:] = (filt_re * v_im + filt_im * v_re).astype(BF16)


def inverse_kernel(devices, line_count, first_row, rows, chunk_count, me_ref, inv_ref, _, *rest):
    spectra, outs = rest[:chunk_count], rest[chunk_count:]
    pieces = []
    for step in range(devices):
        target = lax.rem(me_ref[0] + step, devices)
        start = pl.multiple_of(target * line_count + first_row, PACK)
        pieces.append(inv_ref[pl.ds(start, rows), :])
    left = jnp.concatenate(pieces, axis=0)
    total = outs[0].shape[1] // 2
    width = total // chunk_count
    for chunk in range(chunk_count):
        product = jnp.dot(left, spectra[chunk][...], preferred_element_type=F32).astype(BF16)
        for step in range(devices):
            part = product[step * rows : (step + 1) * rows]
            first = chunk * width
            outs[step][:, first : first + width] = part[:, :width]
            first += total
            outs[step][:, first : first + width] = part[:, width:]


def join_kernel(devices, has_first, has_last, me_ref, _before, _passed, *rest):
    blocks, out_ref = rest[:devices], rest[devices]
    rows, width = blocks[0].shape[0], blocks[0].shape[1] // 2
    samples = out_ref.shape[1] // 2
    for step in range(devices):
        source = lax.rem(me_ref[0] + (devices - step), devices)
        for part in range(2):
            start = pl.multiple_of(part * samples + source * width, LANES)
            out_ref[:, pl.ds(start, width)] = blocks[step][:, part * width : (part + 1) * width]

    def clear(first, low, high):
        edge = out_ref[first : first + PACK, :].astype(F32)
        ids = lax.broadcasted_iota(jnp.int32, edge.shape, 0)
        edge = jnp.where((ids >= low) & (ids < high), 0.0, edge)
        out_ref[first : first + PACK, :] = edge.astype(BF16)

    if has_first:

        @pl.when(me_ref[0] == 0)
        def _():
            clear(0, 0, RIM)

    if has_last:

        @pl.when(me_ref[0] == devices - 1)
        def _():
            clear(rows - PACK, PACK - RIM, PACK)


def coherence_kernel(has_before, *refs):
    dates = SPAN + 1
    now = refs[:dates]
    position = dates
    before = None
    if has_before:
        before = refs[position : position + dates]
        position += dates + 2
    image_ref, result_ref, token_ref, sums_ref = refs[position : position + 4]
    token_ref[...] = jnp.zeros(token_ref.shape, F32)
    lines = image_ref.shape[1]
    samples = image_ref.shape[2]
    window = lines + 2 * RIM
    half_az, half_rg = WIN_AZ // 2, WIN_RG // 2
    block = min(samples, 256)
    terms = 1 + 3 * SPAN
    out_id = lax.broadcasted_iota(jnp.int32, (lines, window), 0)
    in_id = lax.broadcasted_iota(jnp.int32, (lines, window), 1) - RIM
    down = jnp.where(jnp.abs(in_id - out_id) <= half_az, 1.0, 0.0).astype(BF16)
    down = jnp.concatenate([down, down], axis=1)
    size = block + 2 * LANES
    in_id = lax.broadcasted_iota(jnp.int32, (size, block), 0) - LANES
    out_id = lax.broadcasted_iota(jnp.int32, (size, block), 1)
    across = jnp.where(jnp.abs(in_id - out_id) <= half_rg, 1.0, 0.0).astype(BF16)

    def halves(value):
        high = value.astype(BF16)
        return high, (value - high.astype(F32)).astype(BF16)

    def load(date, start):
        piece = now[date][:, pl.ds(start, block)]
        if has_before:
            held = before[date]
            piece = jnp.concatenate(
                [held[held.shape[0] - 2 * RIM :, pl.ds(start, block)], piece], axis=0
            )
        return piece.astype(F32)

    def add_lines(value, term, start):
        both = jnp.concatenate(halves(value), axis=0)
        total = jnp.dot(down, both, preferred_element_type=F32)
        rows = slice(term * lines, (term + 1) * lines)
        for half, part in enumerate(halves(total)):
            sums_ref[half, rows, pl.ds(start + LANES, block)] = part

    edge = jnp.zeros((terms * lines, LANES), BF16)
    for half in range(2):
        sums_ref[half, :, :LANES] = edge
        sums_ref[half, :, samples + LANES :] = edge

    def first_pass(index, _):
        start = pl.multiple_of(index * block, block)
        re = load(0, start)
        im = load(0, samples + start)
        image_ref[0, :, pl.ds(start, block)] = re[RIM : RIM + lines].astype(BF16)
        image_ref[1, :, pl.ds(start, block)] = im[RIM : RIM + lines].astype(BF16)
        add_lines(re * re + im * im, 0, start)
        for date in range(1, dates):
            other_re = load(date, start)
            other_im = load(date, samples + start)
            term = 3 * date - 2
            add_lines(re * other_re + im * other_im, term, start)
            add_lines(im * other_re - re * other_im, term + 1, start)
            add_lines(other_re * other_re + other_im * other_im, term + 2, start)
        return 0

    lax.fori_loop(0, samples // block, first_pass, 0, unroll=2)

    def second_pass(index, _):
        start = pl.multiple_of(index * block, block)
        total = jnp.dot(sums_ref[0, :, pl.ds(start, size)], across, preferred_element_type=F32)
        total += jnp.dot(sums_ref[1, :, pl.ds(start, size)], across, preferred_element_type=F32)

        def box(term):
            return total[term * lines : (term + 1) * lines]

        own = box(0)
        for date in range(1, dates):
            term = 3 * date - 2
            scale = lax.rsqrt(own * box(term + 2) + epsilon)
            result_ref[date - 1, 0, :, pl.ds(start, block)] = (box(term) * scale).astype(BF16)
            result_ref[date - 1, 1, :, pl.ds(start, block)] = (box(term + 1) * scale).astype(BF16)
        return 0

    lax.fori_loop(0, samples // block, second_pass, 0, unroll=2)


def kernel_taps(fraction):
    half_taps = TAPS // 2
    position = jnp.arange(TAPS, dtype=jnp.int32).astype(F32) - (half_taps - 1) - fraction
    return jnp.sinc(position) * (0.5 + 0.5 * jnp.cos(math.pi * position / half_taps))


def scatter(blocks, axis):
    count = lax.axis_size(axis)
    moved = [blocks[0]]
    for step in range(1, count):
        route = [(i, (i + step) % count) for i in range(count)]
        moved.append(lax.ppermute(blocks[step], axis, route))
    return moved


def from_next(block, axis):
    count = lax.axis_size(axis)
    return lax.ppermute(block, axis, [((i + 1) % count, i) for i in range(count)])


def body(raw_echo, range_rate, azimuth_rate, line_offset, frac_shift):
    devices = lax.axis_size("swath")
    lines, samples = raw_echo.shape[2], raw_echo.shape[3]
    size = lines * devices
    half = size // 2
    owned = azimuth_rate.shape[0]
    pulse_len = samples // 2
    me = lax.axis_index("swath").astype(jnp.int32).reshape(1)
    echo = raw_echo.reshape(2 * lines, samples)

    chunk_count = max(1, min(4, owned // LANES))
    width = owned // chunk_count
    depth = pulse_len + width
    block_type = jax.ShapeDtypeStruct((lines, 2 * width), BF16)
    table, *blocks = pl.pallas_call(
        functools.partial(first_range_kernel, devices, pulse_len),
        out_shape=[jax.ShapeDtypeStruct((depth, 2 * width), BF16)] + [block_type] * devices,
        in_specs=[smem(), smem(), vmem()],
        out_specs=[vmem()] * (devices + 1),
        scratch_shapes=[pltpu.VMEM((2, PACK, pulse_len + 2 * width + LANES), F32)],
        compiler_params=params(40),
        cost_estimate=cost(2),
        name="range_first",
    )(me, range_rate.reshape(1), echo)
    columns = []
    for chunk in range(chunk_count):
        if chunk > 0:
            blocks = pl.pallas_call(
                functools.partial(next_range_kernel, devices, chunk, pulse_len),
                out_shape=[block_type] * devices,
                in_specs=[smem(), vmem(), vmem(), hold()],
                out_specs=[vmem()] * devices,
                compiler_params=params(40),
                cost_estimate=cost(1.5),
                name="range_next",
            )(me, echo, table, blocks[0])
        with jax.named_scope(f"columns_{chunk}"):
            columns.append(scatter(blocks, "swath"))

    taps = kernel_taps(frac_shift[0])
    signs = 1.0 - 2.0 * ((line_offset[0] + jnp.arange(TAPS, dtype=jnp.int32)) % 2).astype(F32)
    taps = jnp.concatenate([taps, jnp.sum(taps * signs).reshape(1)])
    dft, inv, coef, filt = pl.pallas_call(
        tables_kernel,
        out_shape=[
            jax.ShapeDtypeStruct((size, size), BF16),
            jax.ShapeDtypeStruct((size + 2 * RIM, size), BF16),
            jax.ShapeDtypeStruct((3, half, LANES), F32),
            jax.ShapeDtypeStruct((2, half + RIM, owned), F32),
        ],
        in_specs=[smem(), smem(), vmem(), hold()],
        out_specs=[vmem()] * 4,
        compiler_params=params(40),
        cost_estimate=cost(8.5),
        name="azimuth_tables",
    )(line_offset, taps, azimuth_rate.reshape(1, owned), blocks[0])

    spectra = []
    for chunk in range(chunk_count):
        spectra.append(
            pl.pallas_call(
                functools.partial(forward_kernel, devices, chunk),
                out_shape=jax.ShapeDtypeStruct((size, 2 * width), BF16),
                in_specs=[smem()] + [vmem()] * 3 + [hold()] + [vmem()] * devices,
                out_specs=vmem(),
                scratch_shapes=[pltpu.VMEM((size, 2 * width), BF16)],
                compiler_params=params(40),
                cost_estimate=cost(1),
                name="azimuth_forward",
            )(me, dft, coef, filt, spectra[-1] if spectra else coef, *columns[chunk])
        )

    step_lines = min(lines, LINE_STEP)
    steps = lines // step_lines
    image = result = held = outs = own = None
    passed = []
    for step in range(steps):
        rows = step_lines + (2 * RIM if step == 0 else 0)
        first_row = step * step_lines + (0 if step == 0 else 2 * RIM)
        outs = pl.pallas_call(
            functools.partial(inverse_kernel, devices, lines, first_row, rows, chunk_count),
            out_shape=[jax.ShapeDtypeStruct((rows, 2 * owned), BF16)] * devices,
            in_specs=[smem(), vmem(), hold()] + [vmem()] * chunk_count,
            out_specs=[vmem()] * devices,
            compiler_params=params(40),
            cost_estimate=cost(0.8),
            name="azimuth_inverse",
        )(me, inv, outs[0] if outs else spectra[-1], *spectra)
        with jax.named_scope(f"strips_{step}"):
            strips = scatter(outs, "swath")
        own = pl.pallas_call(
            functools.partial(join_kernel, devices, step == 0, step == steps - 1),
            out_shape=jax.ShapeDtypeStruct((rows, 2 * samples), BF16),
            in_specs=[smem(), hold(), hold()] + [vmem()] * devices,
            out_specs=vmem(),
            compiler_params=params(40),
            cost_estimate=cost(0.3),
            name="join_strips",
        )(me, own if step else me, passed[step - 2] if step > 1 else me, *strips)
        now = [own]
        for span in range(SPAN):
            with jax.named_scope(f"date_{step}_{span}"):
                now.append(from_next(now[-1], "date"))
        operands = list(now)
        in_specs = [vmem()] * len(now)
        aliases = {}
        if held is not None:
            operands += held + [image, result]
            in_specs += [vmem()] * len(held) + [pl.BlockSpec(memory_space=pl.ANY)] * 2
            aliases = {len(operands) - 2: 0, len(operands) - 1: 1}
        image, result, token = pl.pallas_call(
            functools.partial(coherence_kernel, held is not None),
            grid=(1,),
            out_shape=[
                jax.ShapeDtypeStruct((2, lines, samples), BF16),
                jax.ShapeDtypeStruct((SPAN, 2, lines, samples), BF16),
                jax.ShapeDtypeStruct((8, LANES), F32),
            ],
            in_specs=in_specs,
            out_specs=[
                pl.BlockSpec((2, step_lines, samples), lambda i, s=step: (0, s, 0)),
                pl.BlockSpec((SPAN, 2, step_lines, samples), lambda i, s=step: (0, 0, s, 0)),
                pl.BlockSpec((8, LANES), lambda i: (0, 0)),
            ],
            scratch_shapes=[
                pltpu.VMEM((2, (1 + 3 * SPAN) * step_lines, samples + 2 * LANES), BF16)
            ],
            input_output_aliases=aliases,
            compiler_params=params(48),
            cost_estimate=cost(6),
            name="coherence",
        )(*operands)
        held = now
        passed.append(token)
    return (image[None], result[None])


def solution(mesh):
    placed = (P("date", None, "swath", None), P(), P("swath"), P("date"), P("date"))
    return jax.shard_map(
        body,
        mesh=mesh,
        in_specs=placed,
        out_specs=(P("date", None, "swath", None), P("date", None, None, "swath", None)),
        check_vma=False,
    )
```

```python
import functools
import math

import jax
import jax.numpy as jnp
from jax import lax
from jax.experimental import pallas as pl
from jax.experimental.pallas import tpu as pltpu
from jax.sharding import PartitionSpec as P

TAPS = 8
WIN_AZ = 11
WIN_RG = 5
SPAN = 2
LANES = 128
PACK = 16
RIM = 8
COLUMN_PARTS = (1, 1, 1, 1)
LINE_PARTS = (5, 5, 4, 2)
JOIN_COST = 0.5
COH_COST = 5.0
HOP_WAITS = False
LATER = 0
LAG = 2
PACE = 1.0

two_pi = 2.0 * math.pi
epsilon = 1e-06
F32 = jnp.float32
BF16 = jnp.bfloat16


def params(mib):
    return pltpu.CompilerParams(vmem_limit_bytes=mib * 1024 * 1024)


def cost(micros):
    return pl.CostEstimate(flops=int(micros * PACE * 1e9), bytes_accessed=0, transcendentals=0)


def vmem():
    return pl.BlockSpec(memory_space=pltpu.VMEM)


def hold():
    return pl.BlockSpec(memory_space=pl.ANY)


def smem():
    return pl.BlockSpec(memory_space=pltpu.SMEM)


def sincos_turns(turns):
    quarter = jnp.floor(turns * 4.0 + 0.5)
    x = (turns - quarter * 0.25) * two_pi
    x2 = x * x
    s = x * (1.0 + x2 * (-1.0 / 6 + x2 * (1.0 / 120 + x2 * (-1.0 / 5040 + x2 * (1.0 / 362880)))))
    c = 1.0 + x2 * (-0.5 + x2 * (1.0 / 24 + x2 * (-1.0 / 720 + x2 * (1.0 / 40320))))
    quad = quarter.astype(jnp.int32) & 3
    odd = (quad & 1) == 1
    sin_v = jnp.where(odd, c, s)
    cos_v = jnp.where(odd, s, c)
    sin_v = jnp.where(quad >= 2, -sin_v, sin_v)
    cos_v = jnp.where((quad == 1) | (quad == 2), -cos_v, cos_v)
    return sin_v, cos_v


def build_chirp(rate_ref, table_ref, base_ref, pulse_len, width):
    top = pulse_len + width - PACK
    span = base_ref.shape[2]
    lag = (
        lax.broadcasted_iota(jnp.int32, (PACK, span), 0)
        + top
        - lax.broadcasted_iota(jnp.int32, (PACK, span), 1)
    )
    inside = (lag >= 0) & (lag < pulse_len)
    offset = (lag.astype(F32) - 0.5 * pulse_len) / pulse_len
    turns = 0.5 * pulse_len * rate_ref[0] * offset * offset
    sin_v, cos_v = sincos_turns(turns)
    amplitude = 1.0 / math.sqrt(pulse_len)
    base_ref[0] = jnp.where(inside, cos_v * amplitude, 0.0)
    base_ref[1] = jnp.where(inside, -sin_v * amplitude, 0.0)
    for block in range((pulse_len + width) // PACK):
        start = top - PACK * block
        aligned = start // LANES * LANES
        skew = start - aligned
        size = width + LANES
        for part in range(2):
            window = base_ref[part, :, aligned : aligned + size]
            if skew:
                window = pltpu.roll(window, size - skew, 1)
            table_ref[block * PACK : (block + 1) * PACK, part * width : (part + 1) * width] = (
                window[:, :width].astype(BF16)
            )


def range_blocks(me_ref, echo_ref, table, outs, offset, devices, pulse_len):
    lines = echo_ref.shape[0] // 2
    samples = echo_ref.shape[1]
    width = outs[0].shape[1] // 2
    lane_blocks = samples // LANES
    window_blocks = pulse_len // LANES + 1
    for step in range(devices):
        target = lax.rem(me_ref[0] + step, devices)
        for part in range(width // LANES):
            first = target * (lane_blocks // devices) + offset // LANES + part
            pieces = [
                echo_ref[
                    :,
                    pl.ds(pl.multiple_of(lax.rem(first + j, lane_blocks) * LANES, LANES), LANES),
                ]
                for j in range(window_blocks)
            ]
            window = jnp.concatenate(pieces, axis=1)
            product = jnp.dot(window, table, preferred_element_type=F32)
            real = product[:lines, :LANES] - product[lines:, LANES:]
            imag = product[lines:, :LANES] + product[:lines, LANES:]
            left = part * LANES
            outs[step][:, left : left + LANES] = real.astype(BF16)
            outs[step][:, width + left : width + left + LANES] = imag.astype(BF16)


def first_range_kernel(devices, pulse_len, me_ref, rate_ref, echo_ref, table_ref, *rest):
    outs, base_ref = rest[:-1], rest[-1]
    build_chirp(rate_ref, table_ref, base_ref, pulse_len, LANES)
    range_blocks(me_ref, echo_ref, table_ref[...], outs, 0, devices, pulse_len)


def next_range_kernel(devices, offset, pulse_len, me_ref, echo_ref, table_ref, _, *outs):
    range_blocks(me_ref, echo_ref, table_ref[...], outs, offset, devices, pulse_len)


def tables_kernel(
    shift_ref, taps_ref, rate_ref, _, dft_ref, inv_ref, coef_ref, filt_ref
):
    size = dft_ref.shape[0]
    half = size // 2
    amplitude = 1.0 / math.sqrt(size)
    rows = lax.broadcasted_iota(jnp.int32, (PACK, LANES), 0)
    lanes = lax.broadcasted_iota(jnp.int32, (PACK, LANES), 1)
    period = size // LANES
    turn_of = []
    for block in range(period):
        sin_b, cos_b = sincos_turns(((rows * block) % period).astype(F32) / period)
        turn_of.append((sin_b * amplitude, cos_b * amplitude))

    def base_of(ids):
        return sincos_turns(((ids * lanes) & (size - 1)).astype(F32) / size)

    def alternate(ids):
        return jnp.where((ids & 1) == 0, amplitude, -amplitude)

    def dft_rows(tile, _):
        ids = rows + tile * PACK
        sin_0, cos_0 = base_of(ids)
        row = pl.multiple_of(tile * PACK, PACK)
        for block in range(period):
            sin_b, cos_b = turn_of[block]
            cols = slice(block * LANES, (block + 1) * LANES)
            dft_ref[pl.ds(row, PACK), cols] = (cos_0 * cos_b - sin_0 * sin_b).astype(BF16)
            sin_v = sin_0 * cos_b + cos_0 * sin_b
            sin_v = jnp.where(ids == 0, alternate(lanes), sin_v)
            dft_ref[pl.ds(half + row, PACK), cols] = sin_v.astype(BF16)
        return 0

    lax.fori_loop(0, half // PACK, dft_rows, 0)

    def inv_rows(tile, _):
        ids = rows + (tile * PACK - RIM)
        sin_0, cos_0 = base_of(ids)
        row = pl.multiple_of(tile * PACK, PACK)
        for block in range(half // LANES):
            sin_b, cos_b = turn_of[block]
            cos_v = cos_0 * cos_b - sin_0 * sin_b
            sin_v = sin_0 * cos_b + cos_0 * sin_b
            if block == 0:
                sin_v = jnp.where(lanes == 0, alternate(ids), sin_v)
            first = block * LANES
            inv_ref[pl.ds(row, PACK), first : first + LANES] = cos_v.astype(BF16)
            first += half
            inv_ref[pl.ds(row, PACK), first : first + LANES] = sin_v.astype(BF16)
        return 0

    lax.fori_loop(0, inv_ref.shape[0] // PACK, inv_rows, 0)

    shift = shift_ref[0]

    def coef_rows(tile, _):
        ids = rows + tile * PACK
        row = pl.multiple_of(tile * PACK, PACK)
        sin_v, cos_v = sincos_turns(((ids * shift) & (size - 1)).astype(F32) / size)
        sin_1, cos_1 = sincos_turns(ids.astype(F32) / size)
        sum_c = taps_ref[0] * cos_v
        sum_s = taps_ref[0] * sin_v
        for tap in range(1, TAPS):
            sin_v, cos_v = sin_v * cos_1 + cos_v * sin_1, cos_v * cos_1 - sin_v * sin_1
            sum_c = sum_c + taps_ref[tap] * cos_v
            sum_s = sum_s + taps_ref[tap] * sin_v
        first = ids == 0
        coef_ref[0, pl.ds(row, PACK), :] = jnp.where(first, sum_c, 2.0 * sum_c)
        coef_ref[1, pl.ds(row, PACK), :] = 2.0 * sum_s
        coef_ref[2, pl.ds(row, PACK), :] = jnp.where(first, taps_ref[TAPS], 2.0 * sum_c)
        return 0

    lax.fori_loop(0, half // PACK, coef_rows, 0)

    width = rate_ref.shape[1]
    rate = rate_ref[...]

    def filter_rows(tile, _):
        ids = lax.broadcasted_iota(jnp.int32, (RIM, width), 0) + tile * RIM
        row = pl.multiple_of(tile * RIM, RIM)
        centered = jnp.minimum(ids, half).astype(F32) / size
        sin_v, cos_v = sincos_turns(0.5 * size * rate * centered * centered)
        filt_ref[0, pl.ds(row, RIM), :] = cos_v
        filt_ref[1, pl.ds(row, RIM), :] = sin_v
        return 0

    lax.fori_loop(0, half // RIM + 1, filter_rows, 0)


def forward_kernel(devices, offset, me_ref, dft_ref, coef_ref, filt_ref, _, *rest):
    blocks, out_ref, joined = rest[:devices], rest[devices], rest[devices + 1]
    size = dft_ref.shape[0]
    half = size // 2
    lines, width = blocks[0].shape[0], blocks[0].shape[1] // 2
    for step in range(devices):
        source = lax.rem(me_ref[0] + (devices - step), devices)
        joined[pl.ds(pl.multiple_of(source * lines, lines), lines), :] = blocks[step][...]
    columns = joined[...]
    tile = min(half, 128)
    copies = width // LANES
    for first in range(0, half, tile):
        rows = slice(first, first + tile)
        even = jnp.dot(dft_ref[rows, :], columns, preferred_element_type=F32)
        odd = jnp.dot(
            dft_ref[half + first : half + first + tile, :], columns, preferred_element_type=F32
        )
        coefs = [coef_ref[i, rows, :] for i in range(3)]
        if copies > 1:
            coefs = [jnp.concatenate([value] * copies, axis=1) for value in coefs]
        even_re, even_im = even[:, :width], even[:, width:]
        odd_re, odd_im = odd[:, :width], odd[:, width:]
        u_re = coefs[0] * even_re + coefs[1] * odd_re
        u_im = coefs[0] * even_im + coefs[1] * odd_im
        v_re = coefs[2] * odd_re - coefs[1] * even_re
        v_im = coefs[2] * odd_im - coefs[1] * even_im
        cols = slice(offset, offset + width)
        filt_re, filt_im = filt_ref[0, rows, cols], filt_ref[1, rows, cols]
        out_ref[rows, :width] = (filt_re * u_re - filt_im * u_im).astype(BF16)
        out_ref[rows, width:] = (filt_re * u_im + filt_im * u_re).astype(BF16)
        if first == 0:
            top = lax.broadcasted_iota(jnp.int32, (tile, width), 0) == 0
            filt_re = jnp.where(top, filt_ref[0, half : half + 1, cols], filt_re)
            filt_im = jnp.where(top, filt_ref[1, half : half + 1, cols], filt_im)
        rows = slice(half + first, half + first + tile)
        out_ref[rows, :width] = (filt_re * v_re - filt_im * v_im).astype(BF16)
        out_ref[rows, width:] = (filt_re * v_im + filt_im * v_re).astype(BF16)


def inverse_kernel(devices, line_count, pieces, widths, me_ref, inv_ref, _, *rest):
    spectra, outs = rest[: len(widths)], rest[len(widths) :]
    total = sum(widths)
    for piece, (first_row, rows) in enumerate(pieces):
        left = []
        for step in range(devices):
            target = lax.rem(me_ref[0] + step, devices)
            start = pl.multiple_of(target * line_count + first_row, PACK)
            left.append(inv_ref[pl.ds(start, rows), :])
        left = jnp.concatenate(left, axis=0)
        offset = 0
        for spectrum, width in zip(spectra, widths):
            product = jnp.dot(left, spectrum[...], preferred_element_type=F32).astype(BF16)
            for step in range(devices):
                part = product[step * rows : (step + 1) * rows]
                out = outs[piece * devices + step]
                out[:, offset : offset + width] = part[:, :width]
                out[:, total + offset : total + offset + width] = part[:, width:]
            offset += width


def join_kernel(devices, has_first, has_last, me_ref, _before, _ahead, _ended, *rest):
    blocks, out_ref = rest[:devices], rest[devices]
    rows, width = blocks[0].shape[0], blocks[0].shape[1] // 2
    samples = out_ref.shape[1] // 2
    for step in range(devices):
        source = lax.rem(me_ref[0] + (devices - step), devices)
        for part in range(2):
            start = pl.multiple_of(part * samples + source * width, LANES)
            out_ref[:, pl.ds(start, width)] = blocks[step][:, part * width : (part + 1) * width]

    def clear(first, low, high):
        edge = out_ref[first : first + PACK, :].astype(F32)
        ids = lax.broadcasted_iota(jnp.int32, edge.shape, 0)
        edge = jnp.where((ids >= low) & (ids < high), 0.0, edge)
        out_ref[first : first + PACK, :] = edge.astype(BF16)

    if has_first:

        @pl.when(me_ref[0] == 0)
        def _():
            clear(0, 0, RIM)

    if has_last:

        @pl.when(me_ref[0] == devices - 1)
        def _():
            clear(rows - PACK, PACK - RIM, PACK)


def coherence_kernel(first_line, has_before, _later, *refs):
    dates = SPAN + 1
    now = refs[:dates]
    position = dates
    before = None
    if has_before:
        before = refs[position : position + dates]
        position += dates + 2
    image_out, result_out, token_ref, image_ref, result_ref, sums_ref, sems = refs[position:]
    token_ref[...] = jnp.zeros(token_ref.shape, F32)
    lines = image_ref.shape[1]
    samples = image_ref.shape[2]
    window = lines + 2 * RIM
    half_az, half_rg = WIN_AZ // 2, WIN_RG // 2
    block = min(samples, 256)
    group = min(samples, 512)
    terms = 1 + 3 * SPAN
    out_id = lax.broadcasted_iota(jnp.int32, (lines, window), 0)
    in_id = lax.broadcasted_iota(jnp.int32, (lines, window), 1) - RIM
    down = jnp.where(jnp.abs(in_id - out_id) <= half_az, 1.0, 0.0).astype(BF16)
    size = block + 2 * LANES
    in_id = lax.broadcasted_iota(jnp.int32, (size, block), 0) - LANES
    out_id = lax.broadcasted_iota(jnp.int32, (size, block), 1)
    across = jnp.where(jnp.abs(in_id - out_id) <= half_rg, 1.0, 0.0).astype(BF16)

    def load(date, start):
        piece = now[date][:, start : start + block]
        if has_before:
            held = before[date]
            piece = jnp.concatenate(
                [held[held.shape[0] - 2 * RIM :, start : start + block], piece], axis=0
            )
        return piece.astype(F32)

    def add_lines(value, term, start):
        total = jnp.dot(down, value.astype(BF16), preferred_element_type=F32)
        rows = slice(term * lines, (term + 1) * lines)
        sums_ref[rows, start + LANES : start + LANES + block] = total.astype(BF16)

    edge = jnp.zeros((terms * lines, LANES), BF16)
    sums_ref[:, :LANES] = edge
    sums_ref[:, samples + LANES :] = edge
    for start in range(0, samples, block):
        cols = slice(start, start + block)
        re = load(0, start)
        im = load(0, samples + start)
        image_ref[0, :, cols] = re[RIM : RIM + lines].astype(BF16)
        image_ref[1, :, cols] = im[RIM : RIM + lines].astype(BF16)
        add_lines(re * re + im * im, 0, start)
        for date in range(1, dates):
            other_re = load(date, start)
            other_im = load(date, samples + start)
            term = 3 * date - 2
            add_lines(re * other_re + im * other_im, term, start)
            add_lines(im * other_re - re * other_im, term + 1, start)
            add_lines(other_re * other_re + other_im * other_im, term + 2, start)

    placed = pl.ds(first_line, lines)
    copies = [pltpu.make_async_copy(image_ref, image_out.at[:, placed, :], sems.at[0])]
    copies[0].start()
    for start in range(0, samples, block):
        cols = slice(start, start + block)
        total = jnp.dot(sums_ref[:, start : start + size], across, preferred_element_type=F32)

        def box(term):
            return total[term * lines : (term + 1) * lines]

        own = box(0)
        for date in range(1, dates):
            term = 3 * date - 2
            scale = lax.rsqrt(own * box(term + 2) + epsilon)
            result_ref[date - 1, 0, :, cols] = (box(term) * scale).astype(BF16)
            result_ref[date - 1, 1, :, cols] = (box(term + 1) * scale).astype(BF16)
        if (start + block) % group == 0:
            lanes = pl.ds(start + block - group, group)
            copies.append(
                pltpu.make_async_copy(
                    result_ref.at[:, :, :, lanes],
                    result_out.at[:, :, placed, lanes],
                    sems.at[len(copies)],
                )
            )
            copies[-1].start()
    for copy in copies:
        copy.wait()


def kernel_taps(fraction):
    half_taps = TAPS // 2
    position = jnp.arange(TAPS, dtype=jnp.int32).astype(F32) - (half_taps - 1) - fraction
    return jnp.sinc(position) * (0.5 + 0.5 * jnp.cos(math.pi * position / half_taps))


def scatter(blocks, axis):
    count = lax.axis_size(axis)
    moved = [blocks[0]]
    for step in range(1, count):
        route = [(i, (i + step) % count) for i in range(count)]
        moved.append(lax.ppermute(blocks[step], axis, route))
    return moved


def from_next(block, axis):
    count = lax.axis_size(axis)
    return lax.ppermute(block, axis, [((i + 1) % count, i) for i in range(count)])


def split(total, parts, unit):
    share = total // sum(parts)
    if share * sum(parts) != total or share % unit:
        return [total]
    return [part * share for part in parts]


def wait_for(block, other):
    return pl.pallas_call(
        lambda *refs: None,
        out_shape=jax.ShapeDtypeStruct(block.shape, block.dtype),
        in_specs=[vmem(), hold()],
        out_specs=vmem(),
        input_output_aliases={0: 0},
        compiler_params=params(1),
        cost_estimate=cost(0.1),
        name="wait_for",
    )(block, other)


def more_hops(block, step):
    others = []
    for span in range(1, SPAN):
        with jax.named_scope(f"date_{step}_{span}"):
            block = from_next(block, "date")
        others.append(block)
    return others


def finish(count, first_line, now, held, image, result, later):
    lines, samples = image.shape[1], image.shape[2]
    operands = [later] + list(now)
    in_specs = [hold()] + [vmem()] * len(now)
    aliases = {}
    if held is not None:
        operands += held + [image, result]
        in_specs += [vmem()] * len(held) + [hold()] * 2
        aliases = {len(operands) - 2: 0, len(operands) - 1: 1}
    terms = 1 + 3 * SPAN
    return pl.pallas_call(
        functools.partial(coherence_kernel, first_line, held is not None),
        out_shape=[
            jax.ShapeDtypeStruct(image.shape, BF16),
            jax.ShapeDtypeStruct((SPAN, 2, lines, samples), BF16),
            jax.ShapeDtypeStruct((8, LANES), F32),
        ],
        in_specs=in_specs,
        out_specs=[hold(), hold(), vmem()],
        scratch_shapes=[
            pltpu.VMEM((2, count, samples), BF16),
            pltpu.VMEM((SPAN, 2, count, samples), BF16),
            pltpu.VMEM((terms * count, samples + 2 * LANES), BF16),
            pltpu.SemaphoreType.DMA((1 + max(1, samples // 512),)),
        ],
        input_output_aliases=aliases,
        compiler_params=params(48),
        cost_estimate=cost(COH_COST * count / 64),
        name="coherence",
    )(*operands)


def body(raw_echo, range_rate, azimuth_rate, line_offset, frac_shift):
    devices = lax.axis_size("swath")
    lines, samples = raw_echo.shape[2], raw_echo.shape[3]
    size = lines * devices
    half = size // 2
    owned = azimuth_rate.shape[0]
    pulse_len = samples // 2
    me = lax.axis_index("swath").astype(jnp.int32).reshape(1)
    echo = raw_echo.reshape(2 * lines, samples)

    widths = split(owned, COLUMN_PARTS, LANES)
    depth = pulse_len + LANES
    columns = []
    offset = 0
    blocks = table = None
    for chunk, width in enumerate(widths):
        block_types = [jax.ShapeDtypeStruct((lines, 2 * width), BF16)] * devices
        if chunk == 0:
            table, *blocks = pl.pallas_call(
                functools.partial(first_range_kernel, devices, pulse_len),
                out_shape=[jax.ShapeDtypeStruct((depth, 2 * LANES), BF16)] + block_types,
                in_specs=[smem(), smem(), vmem()],
                out_specs=[vmem()] * (devices + 1),
                scratch_shapes=[pltpu.VMEM((2, PACK, pulse_len + 3 * LANES), F32)],
                compiler_params=params(40),
                cost_estimate=cost(0.5 + 1.3 * width / LANES),
                name="range_first",
            )(me, range_rate.reshape(1), echo)
        else:
            blocks = pl.pallas_call(
                functools.partial(next_range_kernel, devices, offset, pulse_len),
                out_shape=block_types,
                in_specs=[smem(), vmem(), vmem(), hold()],
                out_specs=[vmem()] * devices,
                compiler_params=params(40),
                cost_estimate=cost(0.1 + 1.4 * width / LANES),
                name="range_next",
            )(me, echo, table, blocks[0])
        with jax.named_scope(f"columns_{chunk}"):
            columns.append(scatter(blocks, "swath"))
        offset += width

    taps = kernel_taps(frac_shift[0])
    signs = 1.0 - 2.0 * ((line_offset[0] + jnp.arange(TAPS, dtype=jnp.int32)) % 2).astype(F32)
    taps = jnp.concatenate([taps, jnp.sum(taps * signs).reshape(1)])
    dft, inv, coef, filt = pl.pallas_call(
        tables_kernel,
        out_shape=[
            jax.ShapeDtypeStruct((size, size), BF16),
            jax.ShapeDtypeStruct((size + 2 * RIM, size), BF16),
            jax.ShapeDtypeStruct((3, half, LANES), F32),
            jax.ShapeDtypeStruct((2, half + RIM, owned), F32),
        ],
        in_specs=[smem(), smem(), vmem(), hold()],
        out_specs=[vmem()] * 4,
        compiler_params=params(40),
        cost_estimate=cost(8.5),
        name="azimuth_tables",
    )(line_offset, taps, azimuth_rate.reshape(1, owned), blocks[0])

    spectra = []
    offset = 0
    for chunk, width in enumerate(widths):
        spectra.append(
            pl.pallas_call(
                functools.partial(forward_kernel, devices, offset),
                out_shape=jax.ShapeDtypeStruct((size, 2 * width), BF16),
                in_specs=[smem()] + [vmem()] * 3 + [hold()] + [vmem()] * devices,
                out_specs=vmem(),
                scratch_shapes=[pltpu.VMEM((size, 2 * width), BF16)],
                compiler_params=params(40),
                cost_estimate=cost(0.9 * width / LANES),
                name="azimuth_forward",
            )(me, dft, coef, filt, spectra[-1] if spectra else coef, *columns[chunk])
        )
        offset += width

    line_counts = split(lines, LINE_PARTS, PACK)
    pieces = []
    first_row = 0
    for step, count in enumerate(line_counts):
        rows = count + (2 * RIM if step == 0 else 0)
        pieces.append((first_row, rows))
        first_row += rows

    def invert(chosen, after):
        outs = pl.pallas_call(
            functools.partial(inverse_kernel, devices, lines, chosen, widths),
            out_shape=[
                jax.ShapeDtypeStruct((rows, 2 * owned), BF16)
                for _, rows in chosen
                for _ in range(devices)
            ],
            in_specs=[smem(), vmem(), hold()] + [vmem()] * len(widths),
            out_specs=[vmem()] * (devices * len(chosen)),
            compiler_params=params(40),
            cost_estimate=cost(3.2 * sum(rows for _, rows in chosen) / (lines + 2 * RIM)),
            name="azimuth_inverse",
        )(me, inv, after, *spectra)
        return [outs[i : i + devices] for i in range(0, len(outs), devices)]

    ready = []
    for step in range(min(2, len(pieces))):
        ready += invert([pieces[step]], ready[-1][0] if ready else spectra[-1])
    image = jax.ShapeDtypeStruct((2, lines, samples), BF16)
    state = (image, None, me, None)
    own = hop = None
    stages = []

    def end_step(step, state):
        image, result, _, held = state
        own, hop, others = stages[step]
        now = [own, hop] + others
        later = stages[min(step + LATER, len(stages) - 1)][0] if LATER else me
        image, result, token = finish(
            line_counts[step], sum(line_counts[:step]), now, held, image, result, later
        )
        return image, result, token, now

    for step, (_, rows) in enumerate(pieces):
        with jax.named_scope(f"strips_{step}"):
            strips = scatter(ready[step], "swath")
        last = step == len(pieces) - 1
        own = pl.pallas_call(
            functools.partial(join_kernel, devices, step == 0, last),
            out_shape=jax.ShapeDtypeStruct((rows, 2 * samples), BF16),
            in_specs=[smem()] + [hold()] * 3 + [vmem()] * devices,
            out_specs=vmem(),
            compiler_params=params(40),
            cost_estimate=cost(JOIN_COST),
            name="join_strips",
        )(me, own if step else me, ready[-1][0], state[2], *strips)
        if step + 2 < len(pieces):
            ready += invert([pieces[step + 2]], own)
        if hop is not None:
            if HOP_WAITS:
                hop = wait_for(hop, own)
            stages[-1] = [stages[-1][0], hop, more_hops(hop, step - 1)]
        with jax.named_scope(f"date_{step}_0"):
            hop = from_next(own, "date")
        stages.append([own, hop])
        if step >= LAG:
            state = end_step(step - LAG, state)
    stages[-1].append(more_hops(hop, len(pieces) - 1))
    for step in range(max(0, len(pieces) - LAG), len(pieces)):
        state = end_step(step, state)
    return (state[0][None], state[1][None])


def solution(mesh):
    placed = (P("date", None, "swath", None), P(), P("swath"), P("date"), P("date"))
    return jax.shard_map(
        body,
        mesh=mesh,
        in_specs=placed,
        out_specs=(P("date", None, "swath", None), P("date", None, None, "swath", None)),
        check_vma=False,
    )
```

```python
import functools
import math

import jax
import jax.numpy as jnp
from jax import lax
from jax.experimental import pallas as pl
from jax.experimental.pallas import tpu as pltpu
from jax.sharding import PartitionSpec as P

TAPS = 8
WIN_AZ = 11
WIN_RG = 5
SPAN = 2
LANES = 128
PACK = 16
RIM = 8
COLUMN_PARTS = (1, 1, 1, 1)
LINE_PARTS = (5, 5, 4, 2)
JOIN_COST = 0.5
COH_COST = 5.0
HOP_WAITS = False
LATER = 0
LAG = 2
STEP_SIGN = 1
PACE = 1.0

two_pi = 2.0 * math.pi
epsilon = 1e-06
F32 = jnp.float32
BF16 = jnp.bfloat16


def params(mib):
    return pltpu.CompilerParams(vmem_limit_bytes=mib * 1024 * 1024)


def cost(micros):
    return pl.CostEstimate(flops=int(micros * PACE * 1e9), bytes_accessed=0, transcendentals=0)


def vmem():
    return pl.BlockSpec(memory_space=pltpu.VMEM)


def hold():
    return pl.BlockSpec(memory_space=pl.ANY)


def smem():
    return pl.BlockSpec(memory_space=pltpu.SMEM)


def sincos_turns(turns):
    quarter = jnp.floor(turns * 4.0 + 0.5)
    x = (turns - quarter * 0.25) * two_pi
    x2 = x * x
    s = x * (1.0 + x2 * (-1.0 / 6 + x2 * (1.0 / 120 + x2 * (-1.0 / 5040 + x2 * (1.0 / 362880)))))
    c = 1.0 + x2 * (-0.5 + x2 * (1.0 / 24 + x2 * (-1.0 / 720 + x2 * (1.0 / 40320))))
    quad = quarter.astype(jnp.int32) & 3
    odd = (quad & 1) == 1
    sin_v = jnp.where(odd, c, s)
    cos_v = jnp.where(odd, s, c)
    sin_v = jnp.where(quad >= 2, -sin_v, sin_v)
    cos_v = jnp.where((quad == 1) | (quad == 2), -cos_v, cos_v)
    return sin_v, cos_v


def build_chirp(rate_ref, table_ref, base_ref, pulse_len, width):
    top = pulse_len + width - PACK
    span = base_ref.shape[2]
    lag = (
        lax.broadcasted_iota(jnp.int32, (PACK, span), 0)
        + top
        - lax.broadcasted_iota(jnp.int32, (PACK, span), 1)
    )
    inside = (lag >= 0) & (lag < pulse_len)
    offset = (lag.astype(F32) - 0.5 * pulse_len) / pulse_len
    turns = 0.5 * pulse_len * rate_ref[0] * offset * offset
    sin_v, cos_v = sincos_turns(turns)
    amplitude = 1.0 / math.sqrt(pulse_len)
    base_ref[0] = jnp.where(inside, cos_v * amplitude, 0.0)
    base_ref[1] = jnp.where(inside, -sin_v * amplitude, 0.0)
    for block in range((pulse_len + width) // PACK):
        start = top - PACK * block
        aligned = start // LANES * LANES
        skew = start - aligned
        size = width + LANES
        for part in range(2):
            window = base_ref[part, :, aligned : aligned + size]
            if skew:
                window = pltpu.roll(window, size - skew, 1)
            table_ref[block * PACK : (block + 1) * PACK, part * width : (part + 1) * width] = (
                window[:, :width].astype(BF16)
            )


def range_blocks(me_ref, echo_ref, table, outs, offset, devices, pulse_len):
    lines = echo_ref.shape[0] // 2
    samples = echo_ref.shape[1]
    width = outs[0].shape[1] // 2
    lane_blocks = samples // LANES
    window_blocks = pulse_len // LANES + 1
    for step in range(devices):
        target = lax.rem(me_ref[0] + step, devices)
        for part in range(width // LANES):
            first = target * (lane_blocks // devices) + offset // LANES + part
            pieces = [
                echo_ref[
                    :,
                    pl.ds(pl.multiple_of(lax.rem(first + j, lane_blocks) * LANES, LANES), LANES),
                ]
                for j in range(window_blocks)
            ]
            window = jnp.concatenate(pieces, axis=1)
            product = jnp.dot(window, table, preferred_element_type=F32)
            real = product[:lines, :LANES] - product[lines:, LANES:]
            imag = product[lines:, :LANES] + product[:lines, LANES:]
            left = part * LANES
            outs[step][:, left : left + LANES] = real.astype(BF16)
            outs[step][:, width + left : width + left + LANES] = imag.astype(BF16)


def first_range_kernel(devices, pulse_len, me_ref, rate_ref, echo_ref, table_ref, *rest):
    outs, base_ref = rest[:-1], rest[-1]
    build_chirp(rate_ref, table_ref, base_ref, pulse_len, LANES)
    range_blocks(me_ref, echo_ref, table_ref[...], outs, 0, devices, pulse_len)


def next_range_kernel(devices, offset, pulse_len, me_ref, echo_ref, table_ref, _, *outs):
    range_blocks(me_ref, echo_ref, table_ref[...], outs, offset, devices, pulse_len)


def tables_kernel(
    shift_ref, taps_ref, rate_ref, _, dft_ref, inv_ref, coef_ref, filt_ref
):
    size = dft_ref.shape[0]
    half = size // 2
    amplitude = 1.0 / math.sqrt(size)
    rows = lax.broadcasted_iota(jnp.int32, (PACK, LANES), 0)
    lanes = lax.broadcasted_iota(jnp.int32, (PACK, LANES), 1)
    period = size // LANES
    turn_of = []
    for block in range(period):
        sin_b, cos_b = sincos_turns(((rows * block) % period).astype(F32) / period)
        turn_of.append((sin_b * amplitude, cos_b * amplitude))

    def base_of(ids):
        return sincos_turns(((ids * lanes) & (size - 1)).astype(F32) / size)

    def alternate(ids):
        return jnp.where((ids & 1) == 0, amplitude, -amplitude)

    def dft_rows(tile, _):
        ids = rows + tile * PACK
        sin_0, cos_0 = base_of(ids)
        row = pl.multiple_of(tile * PACK, PACK)
        for block in range(period):
            sin_b, cos_b = turn_of[block]
            cols = slice(block * LANES, (block + 1) * LANES)
            dft_ref[pl.ds(row, PACK), cols] = (cos_0 * cos_b - sin_0 * sin_b).astype(BF16)
            sin_v = sin_0 * cos_b + cos_0 * sin_b
            sin_v = jnp.where(ids == 0, alternate(lanes), sin_v)
            dft_ref[pl.ds(half + row, PACK), cols] = sin_v.astype(BF16)
        return 0

    lax.fori_loop(0, half // PACK, dft_rows, 0)

    def inv_rows(tile, _):
        ids = rows + (tile * PACK - RIM)
        sin_0, cos_0 = base_of(ids)
        row = pl.multiple_of(tile * PACK, PACK)
        for block in range(half // LANES):
            sin_b, cos_b = turn_of[block]
            cos_v = cos_0 * cos_b - sin_0 * sin_b
            sin_v = sin_0 * cos_b + cos_0 * sin_b
            if block == 0:
                sin_v = jnp.where(lanes == 0, alternate(ids), sin_v)
            first = block * LANES
            inv_ref[pl.ds(row, PACK), first : first + LANES] = cos_v.astype(BF16)
            first += half
            inv_ref[pl.ds(row, PACK), first : first + LANES] = sin_v.astype(BF16)
        return 0

    lax.fori_loop(0, inv_ref.shape[0] // PACK, inv_rows, 0)

    shift = shift_ref[0]

    def coef_rows(tile, _):
        ids = rows + tile * PACK
        row = pl.multiple_of(tile * PACK, PACK)
        sin_v, cos_v = sincos_turns(((ids * shift) & (size - 1)).astype(F32) / size)
        sin_1, cos_1 = sincos_turns(ids.astype(F32) / size)
        sum_c = taps_ref[0] * cos_v
        sum_s = taps_ref[0] * sin_v
        for tap in range(1, TAPS):
            sin_v, cos_v = sin_v * cos_1 + cos_v * sin_1, cos_v * cos_1 - sin_v * sin_1
            sum_c = sum_c + taps_ref[tap] * cos_v
            sum_s = sum_s + taps_ref[tap] * sin_v
        first = ids == 0
        coef_ref[0, pl.ds(row, PACK), :] = jnp.where(first, sum_c, 2.0 * sum_c)
        coef_ref[1, pl.ds(row, PACK), :] = 2.0 * sum_s
        coef_ref[2, pl.ds(row, PACK), :] = jnp.where(first, taps_ref[TAPS], 2.0 * sum_c)
        return 0

    lax.fori_loop(0, half // PACK, coef_rows, 0)

    width = rate_ref.shape[1]
    rate = rate_ref[...]

    def filter_rows(tile, _):
        ids = lax.broadcasted_iota(jnp.int32, (RIM, width), 0) + tile * RIM
        row = pl.multiple_of(tile * RIM, RIM)
        centered = jnp.minimum(ids, half).astype(F32) / size
        sin_v, cos_v = sincos_turns(0.5 * size * rate * centered * centered)
        filt_ref[0, pl.ds(row, RIM), :] = cos_v
        filt_ref[1, pl.ds(row, RIM), :] = sin_v
        return 0

    lax.fori_loop(0, half // RIM + 1, filter_rows, 0)


def forward_kernel(devices, offset, me_ref, dft_ref, coef_ref, filt_ref, _, *rest):
    blocks, out_ref, joined = rest[:devices], rest[devices], rest[devices + 1]
    size = dft_ref.shape[0]
    half = size // 2
    lines, width = blocks[0].shape[0], blocks[0].shape[1] // 2
    for step in range(devices):
        source = lax.rem(me_ref[0] + (devices - step), devices)
        joined[pl.ds(pl.multiple_of(source * lines, lines), lines), :] = blocks[step][...]
    columns = joined[...]
    tile = min(half, 128)
    copies = width // LANES
    for first in range(0, half, tile):
        rows = slice(first, first + tile)
        even = jnp.dot(dft_ref[rows, :], columns, preferred_element_type=F32)
        odd = jnp.dot(
            dft_ref[half + first : half + first + tile, :], columns, preferred_element_type=F32
        )
        coefs = [coef_ref[i, rows, :] for i in range(3)]
        if copies > 1:
            coefs = [jnp.concatenate([value] * copies, axis=1) for value in coefs]
        even_re, even_im = even[:, :width], even[:, width:]
        odd_re, odd_im = odd[:, :width], odd[:, width:]
        u_re = coefs[0] * even_re + coefs[1] * odd_re
        u_im = coefs[0] * even_im + coefs[1] * odd_im
        v_re = coefs[2] * odd_re - coefs[1] * even_re
        v_im = coefs[2] * odd_im - coefs[1] * even_im
        cols = slice(offset, offset + width)
        filt_re, filt_im = filt_ref[0, rows, cols], filt_ref[1, rows, cols]
        out_ref[rows, :width] = (filt_re * u_re - filt_im * u_im).astype(BF16)
        out_ref[rows, width:] = (filt_re * u_im + filt_im * u_re).astype(BF16)
        if first == 0:
            top = lax.broadcasted_iota(jnp.int32, (tile, width), 0) == 0
            filt_re = jnp.where(top, filt_ref[0, half : half + 1, cols], filt_re)
            filt_im = jnp.where(top, filt_ref[1, half : half + 1, cols], filt_im)
        rows = slice(half + first, half + first + tile)
        out_ref[rows, :width] = (filt_re * v_re - filt_im * v_im).astype(BF16)
        out_ref[rows, width:] = (filt_re * v_im + filt_im * v_re).astype(BF16)


def inverse_kernel(devices, line_count, pieces, widths, me_ref, inv_ref, _, *rest):
    spectra, outs = rest[: len(widths)], rest[len(widths) :]
    total = sum(widths)
    for piece, (first_row, rows) in enumerate(pieces):
        left = []
        for step in range(devices):
            target = lax.rem(me_ref[0] + step, devices)
            start = pl.multiple_of(target * line_count + first_row, PACK)
            left.append(inv_ref[pl.ds(start, rows), :])
        left = jnp.concatenate(left, axis=0)
        offset = 0
        for spectrum, width in zip(spectra, widths):
            product = jnp.dot(left, spectrum[...], preferred_element_type=F32).astype(BF16)
            for step in range(devices):
                part = product[step * rows : (step + 1) * rows]
                out = outs[piece * devices + step]
                out[:, offset : offset + width] = part[:, :width]
                out[:, total + offset : total + offset + width] = part[:, width:]
            offset += width


def join_kernel(devices, has_first, has_last, me_ref, _before, _ahead, _ended, *rest):
    blocks, out_ref = rest[:devices], rest[devices]
    rows, width = blocks[0].shape[0], blocks[0].shape[1] // 2
    samples = out_ref.shape[1] // 2
    for step in range(devices):
        source = lax.rem(me_ref[0] + (devices - step), devices)
        for part in range(2):
            start = pl.multiple_of(part * samples + source * width, LANES)
            out_ref[:, pl.ds(start, width)] = blocks[step][:, part * width : (part + 1) * width]

    def clear(first, low, high):
        edge = out_ref[first : first + PACK, :].astype(F32)
        ids = lax.broadcasted_iota(jnp.int32, edge.shape, 0)
        edge = jnp.where((ids >= low) & (ids < high), 0.0, edge)
        out_ref[first : first + PACK, :] = edge.astype(BF16)

    if has_first:

        @pl.when(me_ref[0] == 0)
        def _():
            clear(0, 0, RIM)

    if has_last:

        @pl.when(me_ref[0] == devices - 1)
        def _():
            clear(rows - PACK, PACK - RIM, PACK)


def coherence_kernel(first_line, has_before, _later, *refs):
    dates = SPAN + 1
    now = refs[:dates]
    position = dates
    before = None
    if has_before:
        before = refs[position : position + dates]
        position += dates + 2
    image_out, result_out, token_ref, image_ref, result_ref, sums_ref, sems = refs[position:]
    token_ref[...] = jnp.zeros(token_ref.shape, F32)
    lines = image_ref.shape[1]
    samples = image_ref.shape[2]
    window = lines + 2 * RIM
    half_az, half_rg = WIN_AZ // 2, WIN_RG // 2
    block = min(samples, 256)
    group = min(samples, 512)
    terms = 1 + 3 * SPAN
    out_id = lax.broadcasted_iota(jnp.int32, (lines, window), 0)
    in_id = lax.broadcasted_iota(jnp.int32, (lines, window), 1) - RIM
    down = jnp.where(jnp.abs(in_id - out_id) <= half_az, 1.0, 0.0).astype(BF16)
    size = block + 2 * LANES
    in_id = lax.broadcasted_iota(jnp.int32, (size, block), 0) - LANES
    out_id = lax.broadcasted_iota(jnp.int32, (size, block), 1)
    across = jnp.where(jnp.abs(in_id - out_id) <= half_rg, 1.0, 0.0).astype(BF16)

    def load(date, start):
        piece = now[date][:, start : start + block]
        if has_before:
            held = before[date]
            piece = jnp.concatenate(
                [held[held.shape[0] - 2 * RIM :, start : start + block], piece], axis=0
            )
        return piece.astype(F32)

    def add_lines(value, term, start):
        total = jnp.dot(down, value.astype(BF16), preferred_element_type=F32)
        rows = slice(term * lines, (term + 1) * lines)
        sums_ref[rows, start + LANES : start + LANES + block] = total.astype(BF16)

    edge = jnp.zeros((terms * lines, LANES), BF16)
    sums_ref[:, :LANES] = edge
    sums_ref[:, samples + LANES :] = edge
    for start in range(0, samples, block):
        cols = slice(start, start + block)
        re = load(0, start)
        im = load(0, samples + start)
        image_ref[0, :, cols] = re[RIM : RIM + lines].astype(BF16)
        image_ref[1, :, cols] = im[RIM : RIM + lines].astype(BF16)
        add_lines(re * re + im * im, 0, start)
        for date in range(1, dates):
            other_re = load(date, start)
            other_im = load(date, samples + start)
            term = 3 * date - 2
            add_lines(re * other_re + im * other_im, term, start)
            add_lines(im * other_re - re * other_im, term + 1, start)
            add_lines(other_re * other_re + other_im * other_im, term + 2, start)

    placed = pl.ds(first_line, lines)
    copies = [pltpu.make_async_copy(image_ref, image_out.at[:, placed, :], sems.at[0])]
    copies[0].start()
    for start in range(0, samples, block):
        cols = slice(start, start + block)
        total = jnp.dot(sums_ref[:, start : start + size], across, preferred_element_type=F32)

        def box(term):
            return total[term * lines : (term + 1) * lines]

        own = box(0)
        for date in range(1, dates):
            term = 3 * date - 2
            scale = lax.rsqrt(own * box(term + 2) + epsilon)
            result_ref[date - 1, 0, :, cols] = (box(term) * scale).astype(BF16)
            result_ref[date - 1, 1, :, cols] = (box(term + 1) * scale).astype(BF16)
        if (start + block) % group == 0:
            lanes = pl.ds(start + block - group, group)
            copies.append(
                pltpu.make_async_copy(
                    result_ref.at[:, :, :, lanes],
                    result_out.at[:, :, placed, lanes],
                    sems.at[len(copies)],
                )
            )
            copies[-1].start()
    for copy in copies:
        copy.wait()


def kernel_taps(fraction):
    half_taps = TAPS // 2
    position = jnp.arange(TAPS, dtype=jnp.int32).astype(F32) - (half_taps - 1) - fraction
    return jnp.sinc(position) * (0.5 + 0.5 * jnp.cos(math.pi * position / half_taps))


def scatter(blocks, axis):
    count = lax.axis_size(axis)
    moved = [blocks[0]] + [None] * (count - 1)
    for step in sorted(range(1, count), key=lambda step: STEP_SIGN * abs(2 * step - count)):
        route = [(i, (i + step) % count) for i in range(count)]
        moved[step] = lax.ppermute(blocks[step], axis, route)
    return moved


def from_next(block, axis):
    count = lax.axis_size(axis)
    return lax.ppermute(block, axis, [((i + 1) % count, i) for i in range(count)])


def split(total, parts, unit):
    share = total // sum(parts)
    if share * sum(parts) != total or share % unit:
        return [total]
    return [part * share for part in parts]


def wait_for(block, other):
    return pl.pallas_call(
        lambda *refs: None,
        out_shape=jax.ShapeDtypeStruct(block.shape, block.dtype),
        in_specs=[vmem(), hold()],
        out_specs=vmem(),
        input_output_aliases={0: 0},
        compiler_params=params(1),
        cost_estimate=cost(0.1),
        name="wait_for",
    )(block, other)


def more_hops(block, step):
    others = []
    for span in range(1, SPAN):
        with jax.named_scope(f"date_{step}_{span}"):
            block = from_next(block, "date")
        others.append(block)
    return others


def finish(count, first_line, now, held, image, result, later):
    lines, samples = image.shape[1], image.shape[2]
    operands = [later] + list(now)
    in_specs = [hold()] + [vmem()] * len(now)
    aliases = {}
    if held is not None:
        operands += held + [image, result]
        in_specs += [vmem()] * len(held) + [hold()] * 2
        aliases = {len(operands) - 2: 0, len(operands) - 1: 1}
    terms = 1 + 3 * SPAN
    return pl.pallas_call(
        functools.partial(coherence_kernel, first_line, held is not None),
        out_shape=[
            jax.ShapeDtypeStruct(image.shape, BF16),
            jax.ShapeDtypeStruct((SPAN, 2, lines, samples), BF16),
            jax.ShapeDtypeStruct((8, LANES), F32),
        ],
        in_specs=in_specs,
        out_specs=[hold(), hold(), vmem()],
        scratch_shapes=[
            pltpu.VMEM((2, count, samples), BF16),
            pltpu.VMEM((SPAN, 2, count, samples), BF16),
            pltpu.VMEM((terms * count, samples + 2 * LANES), BF16),
            pltpu.SemaphoreType.DMA((1 + max(1, samples // 512),)),
        ],
        input_output_aliases=aliases,
        compiler_params=params(48),
        cost_estimate=cost(COH_COST * count / 64),
        name="coherence",
    )(*operands)


def body(raw_echo, range_rate, azimuth_rate, line_offset, frac_shift):
    devices = lax.axis_size("swath")
    lines, samples = raw_echo.shape[2], raw_echo.shape[3]
    size = lines * devices
    half = size // 2
    owned = azimuth_rate.shape[0]
    pulse_len = samples // 2
    me = lax.axis_index("swath").astype(jnp.int32).reshape(1)
    echo = raw_echo.reshape(2 * lines, samples)

    widths = split(owned, COLUMN_PARTS, LANES)
    depth = pulse_len + LANES
    columns = []
    offset = 0
    blocks = table = None
    for chunk, width in enumerate(widths):
        block_types = [jax.ShapeDtypeStruct((lines, 2 * width), BF16)] * devices
        if chunk == 0:
            table, *blocks = pl.pallas_call(
                functools.partial(first_range_kernel, devices, pulse_len),
                out_shape=[jax.ShapeDtypeStruct((depth, 2 * LANES), BF16)] + block_types,
                in_specs=[smem(), smem(), vmem()],
                out_specs=[vmem()] * (devices + 1),
                scratch_shapes=[pltpu.VMEM((2, PACK, pulse_len + 3 * LANES), F32)],
                compiler_params=params(40),
                cost_estimate=cost(0.5 + 1.3 * width / LANES),
                name="range_first",
            )(me, range_rate.reshape(1), echo)
        else:
            blocks = pl.pallas_call(
                functools.partial(next_range_kernel, devices, offset, pulse_len),
                out_shape=block_types,
                in_specs=[smem(), vmem(), vmem(), hold()],
                out_specs=[vmem()] * devices,
                compiler_params=params(40),
                cost_estimate=cost(0.1 + 1.4 * width / LANES),
                name="range_next",
            )(me, echo, table, blocks[0])
        with jax.named_scope(f"columns_{chunk}"):
            columns.append(scatter(blocks, "swath"))
        offset += width

    taps = kernel_taps(frac_shift[0])
    signs = 1.0 - 2.0 * ((line_offset[0] + jnp.arange(TAPS, dtype=jnp.int32)) % 2).astype(F32)
    taps = jnp.concatenate([taps, jnp.sum(taps * signs).reshape(1)])
    dft, inv, coef, filt = pl.pallas_call(
        tables_kernel,
        out_shape=[
            jax.ShapeDtypeStruct((size, size), BF16),
            jax.ShapeDtypeStruct((size + 2 * RIM, size), BF16),
            jax.ShapeDtypeStruct((3, half, LANES), F32),
            jax.ShapeDtypeStruct((2, half + RIM, owned), F32),
        ],
        in_specs=[smem(), smem(), vmem(), hold()],
        out_specs=[vmem()] * 4,
        compiler_params=params(40),
        cost_estimate=cost(8.5),
        name="azimuth_tables",
    )(line_offset, taps, azimuth_rate.reshape(1, owned), blocks[0])

    spectra = []
    offset = 0
    for chunk, width in enumerate(widths):
        spectra.append(
            pl.pallas_call(
                functools.partial(forward_kernel, devices, offset),
                out_shape=jax.ShapeDtypeStruct((size, 2 * width), BF16),
                in_specs=[smem()] + [vmem()] * 3 + [hold()] + [vmem()] * devices,
                out_specs=vmem(),
                scratch_shapes=[pltpu.VMEM((size, 2 * width), BF16)],
                compiler_params=params(40),
                cost_estimate=cost(0.9 * width / LANES),
                name="azimuth_forward",
            )(me, dft, coef, filt, spectra[-1] if spectra else coef, *columns[chunk])
        )
        offset += width

    line_counts = split(lines, LINE_PARTS, PACK)
    pieces = []
    first_row = 0
    for step, count in enumerate(line_counts):
        rows = count + (2 * RIM if step == 0 else 0)
        pieces.append((first_row, rows))
        first_row += rows

    def invert(chosen, after):
        outs = pl.pallas_call(
            functools.partial(inverse_kernel, devices, lines, chosen, widths),
            out_shape=[
                jax.ShapeDtypeStruct((rows, 2 * owned), BF16)
                for _, rows in chosen
                for _ in range(devices)
            ],
            in_specs=[smem(), vmem(), hold()] + [vmem()] * len(widths),
            out_specs=[vmem()] * (devices * len(chosen)),
            compiler_params=params(40),
            cost_estimate=cost(3.2 * sum(rows for _, rows in chosen) / (lines + 2 * RIM)),
            name="azimuth_inverse",
        )(me, inv, after, *spectra)
        return [outs[i : i + devices] for i in range(0, len(outs), devices)]

    ready = []
    for step in range(min(2, len(pieces))):
        ready += invert([pieces[step]], ready[-1][0] if ready else spectra[-1])
    image = jax.ShapeDtypeStruct((2, lines, samples), BF16)
    state = (image, None, me, None)
    own = hop = None
    stages = []

    def end_step(step, state):
        image, result, _, held = state
        own, hop, others = stages[step]
        now = [own, hop] + others
        later = stages[min(step + LATER, len(stages) - 1)][0] if LATER else me
        image, result, token = finish(
            line_counts[step], sum(line_counts[:step]), now, held, image, result, later
        )
        return image, result, token, now

    for step, (_, rows) in enumerate(pieces):
        with jax.named_scope(f"strips_{step}"):
            strips = scatter(ready[step], "swath")
        last = step == len(pieces) - 1
        own = pl.pallas_call(
            functools.partial(join_kernel, devices, step == 0, last),
            out_shape=jax.ShapeDtypeStruct((rows, 2 * samples), BF16),
            in_specs=[smem()] + [hold()] * 3 + [vmem()] * devices,
            out_specs=vmem(),
            compiler_params=params(40),
            cost_estimate=cost(JOIN_COST),
            name="join_strips",
        )(me, own if step else me, ready[-1][0], state[2], *strips)
        if step + 2 < len(pieces):
            ready += invert([pieces[step + 2]], own)
        if hop is not None:
            if HOP_WAITS:
                hop = wait_for(hop, own)
            stages[-1] = [stages[-1][0], hop, more_hops(hop, step - 1)]
        with jax.named_scope(f"date_{step}_0"):
            hop = from_next(own, "date")
        stages.append([own, hop])
        if step >= LAG:
            state = end_step(step - LAG, state)
    stages[-1].append(more_hops(hop, len(pieces) - 1))
    for step in range(max(0, len(pieces) - LAG), len(pieces)):
        state = end_step(step, state)
    return (state[0][None], state[1][None])


def solution(mesh):
    placed = (P("date", None, "swath", None), P(), P("swath"), P("date"), P("date"))
    return jax.shard_map(
        body,
        mesh=mesh,
        in_specs=placed,
        out_specs=(P("date", None, "swath", None), P("date", None, None, "swath", None)),
        check_vma=False,
    )
```
